512 devices in a mesh: dp: 16 (over y, x_hi, core), slab: 32 (over z, x_lo).
Axes of the slice: x: 4 (x_hi: 2, x_lo: 2; x = x_hi * 2 + x_lo), y: 4, z: 16, core: 2. Of those that a mesh axis runs over, the one named last changes fastest.
Arguments:
- features: bfloat16 [16, 64, 256, 8, 256], P('dp', None, 'slab'), may hold values from -6 to 6
- target: bfloat16 [16, 256, 8, 256], P('dp', 'slab'), may hold values from -6 to 6
- out_weight: float32 [64], replicated, may hold values from -1.5 to 1.5
- rotation: int32 [16], P('dp'), may hold values from 0 to 3
- blocks: int32 [8, 2], replicated, may hold values from 0 to 3, as said below
- wedge: int32 [256, 256], replicated, may hold values 0 or 1
Outputs:
- vol_grad: float32 [16, 256, 8, 256], P('dp', 'slab')
- w_grad: float32 [64], replicated
The draws below stay inside these ranges and needn't reach their ends.
Inputs may be any that keep to these rules, and one draw needn't show every extreme that they name: `blocks`: the 8 rows are distinct pairs of block indices of the frequency plane, each from 0 to 3.
All inputs are finite; a program needn't handle non-finite values.
Results may differ from the reference program's by a relative error of at most 0.0003.
Values sent between devices are 32-bit elements; how exact they have to be, the bound alone decides.
No kernel may reach another device: no remote copies, remote signals or barrier semaphores. Data moves between devices by JAX's collectives and lax.ppermute only.
A program may use at most 64 MiB of HBM per device.

```python
import jax
import jax.numpy as jnp
from jax import lax

C = 64
N = 256
BLK = 64
NB = 8
YP = 8
SAMPLES = 16


def draw_blocks(key, part):
    per_side = N // BLK
    picked = jax.random.permutation(key, per_side * per_side)[:NB]
    return jnp.stack([picked // per_side, picked % per_side], axis=1).astype(jnp.int32)


def place_ends(drawn, stream_key, smallest, top_value):
    longest = drawn.shape.index(max(drawn.shape))
    spots = []
    for shift in (0, 1):
        where = [jax.random.randint(jax.random.fold_in(stream_key, axis), (), 0, length) for axis, length in enumerate(drawn.shape)]
        where[longest] = (where[longest] + shift) % drawn.shape[longest]
        spots.append(tuple(where))
    return drawn.at[spots[0]].set(smallest).at[spots[1]].set(top_value)


def steps_of(own_key, extent, split, low, largest):
    factor_of = 1.0
    for dim, shards_of in split:
        heights = jax.random.uniform(jax.random.fold_in(jax.random.fold_in(own_key, 6), dim), (shards_of,), jnp.float32, low / len(split), largest / len(split))
        factor_of = factor_of * jnp.repeat(jnp.exp(heights), extent[dim] // shards_of).reshape((-1,) + (1,) * (len(extent) - 1 - dim))
    return factor_of


def centred(own_key, dims, deviation, most, cuts=(), kind=jnp.bfloat16):
    values = deviation * jax.random.normal(own_key, dims, jnp.float32)
    if cuts:
        values = values * steps_of(own_key, dims, cuts, -0.22, 0.18)
    return jnp.clip(values, -most, most).astype(kind)


def setup_inputs(seed: int = 0) -> dict:
    streams_of = jax.random.split(jax.random.key(seed), 7)
    return {
        "features": centred(streams_of[0], (SAMPLES, C, N, YP, N), 1.0, 6.0, ((0, 16), (2, 32))),
        "target": centred(streams_of[1], (SAMPLES, N, YP, N), 1.0, 6.0, ((0, 16), (1, 32))),
        "out_weight": centred(streams_of[2], (C,), 0.25, 1.5, (), jnp.float32),
        "rotation": place_ends(jax.random.randint(streams_of[3], (SAMPLES,), 0, 4), jax.random.fold_in(streams_of[3], 1), 0, 3).astype(jnp.int32),
        "blocks": draw_blocks(jax.random.fold_in(streams_of[6], 71), 0),
        "wedge": place_ends((jax.random.randint(streams_of[5], (N, N), 0, 5) < 3).astype(jnp.int32), jax.random.fold_in(streams_of[5], 1), 0, 1),
    }


def turned(volume, turns):
    result = volume
    for count in range(1, 4):
        result = jnp.where(turns == count, jnp.rot90(volume, count, axes=(0, 2)), result)
    return result


def wedge_weights(blocks, wedge):
    per_side = N // BLK
    labels = jnp.arange(per_side, dtype=jnp.int32)
    match = (blocks[:, 0][:, None, None] == labels[None, :, None]) & (blocks[:, 1][:, None, None] == labels[None, None, :])
    listed = jnp.any(match, axis=0)
    spread = jnp.repeat(jnp.repeat(listed, BLK, axis=0), BLK, axis=1)
    return jnp.where(spread, wedge, 0).astype(jnp.float32)


def reference(features, target, out_weight, rotation, blocks, wedge):
    mask = wedge_weights(blocks, wedge)

    def single(items):
        sample, other, turns = items
        wide = sample.astype(jnp.float32)
        volume = jnp.einsum("c,czyx->zyx", out_weight, wide, precision=lax.Precision.HIGHEST)
        difference = volume - other.astype(jnp.float32)
        rotated = turned(difference, turns)
        spectrum = jnp.fft.fft2(rotated, axes=(0, 2)) / N
        grad_spectrum = 2.0 * mask[:, None, :] * spectrum
        rot_grad = N * jnp.real(jnp.fft.ifft2(grad_spectrum, axes=(0, 2)))
        back = turned(rot_grad, (4 - turns) % 4).astype(jnp.float32)
        piece = jnp.einsum("czyx,zyx->c", wide, back, precision=lax.Precision.HIGHEST)
        return back, piece.astype(jnp.float32)

    vol_grad, pieces = lax.map(single, (features, target, rotation))
    w_grad = jnp.sum(pieces, axis=0) / (SAMPLES * N * YP * N)
    return vol_grad, w_grad
```

```python
import functools
import math

import jax
import jax.numpy as jnp
import numpy as np
from jax import lax
from jax.experimental import pallas as pl
from jax.experimental.pallas import tpu as pltpu
from jax.sharding import Mesh
from jax.sharding import PartitionSpec as P

N = 256
C = 64
BLK = 64
NB = 8
SLABS = 32
ZL = 8
YP = 8
ROWS = ZL * YP
CHUNKS = 4
PARTS = {"dp": (("y", 4), ("xh", 2), ("core", 2)), "slab": (("z", 16), ("xl", 2))}
NEAR = ("y", "xh")
FAR = ("core", "z", "xl")

F32, BF16 = jnp.float32, jnp.bfloat16
VMEM_LIMIT = 16 * 1024 * 1024


def halves(table):
    high = table.astype(np.float32).astype(BF16)
    low = (table - high.astype(np.float64)).astype(np.float32).astype(BF16)
    return high, low


def tables():
    step = 2.0 * math.pi / N
    space = np.arange(N)
    quad, slab = np.meshgrid(np.arange(4), np.arange(SLABS), indexing="ij")
    freq = (4 * slab + quad).reshape(-1)
    phase = (freq[:, None] * space[None, :]) % N * step
    real, imag = np.cos(phase), -np.sin(phase)
    imag[freq == 0] = np.cos(math.pi * space)
    forward = np.concatenate([real, imag], 0)
    weight = np.where(freq == 0, 1.0, 2.0)[:, None] / (N * N)
    inverse = np.concatenate([real * weight, imag * weight], 0)
    zp, m, i = np.meshgrid(np.arange(2), np.arange(4), np.arange(SLABS), indexing="ij")
    depth = (8 * i + 2 * m + zp).reshape(-1)
    phase = (space[:, None] * depth[None, :]) % N * step
    along = np.concatenate([np.cos(phase), np.sin(phase)], 0)
    return halves(forward), halves(along), halves(along.T.copy()), halves(inverse)


def split(values):
    high = values.astype(BF16)
    return high, (values - high.astype(F32)).astype(BF16)


def dot(left, right, dims=((1,), (0,))):
    return lax.dot_general(left, right, (dims, ((), ())), preferred_element_type=F32)


def lane_of(shape):
    return lax.broadcasted_iota(jnp.int32, shape, 1)


def regroup(pieces, to):
    group = (lane_of(pieces[0].shape) >> 4) & 3
    result = None
    for source in range(4):
        moved = pieces[source] if source == to else pltpu.roll(pieces[source], (16 * (source - to)) % 128, 1)
        result = moved if result is None else jnp.where(group == source, moved, result)
    return result


def filter_weights(turn, place, blocks, wedge, out):
    kz = lax.broadcasted_iota(jnp.int32, (8, N), 0)
    kx = lane_of((8, N)) >> 6
    listed = jnp.zeros((8, N), jnp.bool_)
    for n in range(NB):
        listed = listed | ((kz == blocks[n, 0]) & (kx == blocks[n, 1]))
    listed = listed.astype(F32)
    mask = jnp.concatenate(
        [wedge[a * BLK : (a + 1) * BLK, :].astype(F32) * listed[a : a + 1, :] for a in range(N // BLK)], 0
    ).astype(BF16)
    lane = lane_of((N, 128))
    row = lax.broadcasted_iota(jnp.int32, (N, 128), 0)
    quad = (lane >> 4) & 3
    freq = 4 * place + quad
    freq = jnp.where((freq == 0) & (lane >= 64), N // 2, freq)
    plus = (row == freq).astype(F32).astype(BF16)
    minus = (row == ((N - freq) & (N - 1))).astype(F32).astype(BF16)
    picks = jnp.concatenate([plus, minus], 1)
    odd = (turn & 1) == 1
    plain = dot(mask, picks)
    other = dot(mask, picks, ((0,), (0,)))
    direct = jnp.where(odd, other[:, 128:], plain[:, :128])
    mirror = jnp.where(odd, other[:, :128], plain[:, 128:]).astype(BF16)
    p = lax.broadcasted_iota(jnp.int32, (N, N), 0)
    s = lane_of((N, N))
    flip = (((p + s) & (N - 1)) == 0).astype(F32).astype(BF16)
    out[...] = direct + dot(flip, mirror)


def forward_x(place, turn, weight, blocks, wedge, features, target, fwd_high, fwd_low, lines, factors, held, sems):
    part = C * ROWS // CHUNKS
    copies = []
    for k in range(CHUNKS):
        rows = pl.ds(k * part, part)
        copies.append(pltpu.make_async_copy(features.at[rows], held.at[rows], sems.at[k]))
        copies[-1].start()
    filter_weights(turn[0], place[0], blocks, wedge, factors)
    total = -target[...].astype(F32)
    for k in range(CHUNKS):
        copies[k].wait()
        for c in range(k * C // CHUNKS, (k + 1) * C // CHUNKS):
            total = total + weight[c] * held[c * ROWS : (c + 1) * ROWS, :].astype(F32)
    high, low = split(total)
    high = jnp.concatenate([high, high], 0)
    low = jnp.concatenate([low, low], 0)
    nt = ((1,), (1,))
    line = dot(fwd_high[...], high, nt) + (dot(fwd_high[...], low, nt) + dot(fwd_low[...], high, nt))
    line = jnp.where(lane_of((128, 128)) < 64, line[:128], line[128:])
    pieces = [line[q * SLABS : (q + 1) * SLABS] for q in range(4)]
    for m in range(4):
        lines[pl.ds(m, SLABS, stride=4), :] = regroup(pieces, m)


def filter_z(place, lines, factors, fwd_high, fwd_low, inv_high, inv_low, back):
    even = jnp.concatenate([lines[pl.ds(m, SLABS, stride=4), :] for m in range(4)], 0)
    data = jnp.concatenate([even, pltpu.roll(even, 120, 1)], 0)
    high, low = split(data)
    freq = dot(fwd_high[...], high) + (dot(fwd_high[...], low) + dot(fwd_low[...], high))
    cosine, sine = freq[:N], freq[N:]
    lane = lane_of((N, 128))
    sign = jnp.where(lane < 64, 1.0, -1.0)
    sign = jnp.where((place[0] == 0) & (((lane >> 4) & 3) == 0), 0.0, sign)
    scale = factors[...]
    kept_cosine = scale * (cosine + sign * pltpu.roll(sine, 64, 1))
    kept_sine = scale * (sine - sign * pltpu.roll(cosine, 64, 1))
    high, low = split(jnp.concatenate([kept_cosine, kept_sine], 0))
    depth = dot(inv_high[...], high) + (dot(inv_high[...], low) + dot(inv_low[...], high))
    lane = lane_of((SLABS, 128))
    for m in range(4):
        first = depth[m * SLABS : (m + 1) * SLABS]
        second = depth[128 + m * SLABS : 128 + (m + 1) * SLABS]
        back[pl.ds(m, SLABS, stride=4), :] = jnp.where((lane & 8) == 0, first, pltpu.roll(second, 8, 1))


def inverse_x(lines, features, inv_high, inv_low, volume, sums, partial):
    blocks = [lines[pl.ds(m, SLABS, stride=4), :] for m in range(4)]
    line = jnp.concatenate([regroup(blocks, q) for q in range(4)], 0).T
    line = jnp.concatenate([line[:64], line[64:]], 1)
    high, low = split(line)
    result = dot(high, inv_high[...]) + (dot(low, inv_high[...]) + dot(high, inv_low[...]))
    volume[...] = result

    def channels(step, carry):
        for k in range(8):
            c = step * 8 + k
            piece = features[pl.ds(pl.multiple_of(c * ROWS, ROWS), ROWS), :].astype(F32) * result
            piece = sum(piece[z * YP : (z + 1) * YP] for z in range(ZL))
            partial[pl.ds(pl.multiple_of(c * YP, YP), YP), :] = piece[:, :128] + piece[:, 128:]
        return carry

    lax.fori_loop(0, C // 8, channels, 0)
    total = sum(partial[pl.ds(y, C, stride=YP), :] for y in range(YP))
    total = jnp.concatenate([total, jnp.zeros((128 - C, 128), F32)], 0)
    high, low = split(total)
    rest = (total - high.astype(F32) - low.astype(F32)).astype(BF16)
    ones = jnp.ones((sums.shape[0], 128), BF16)
    nt = ((1,), (1,))
    sums[...] = dot(ones, high, nt) + (dot(ones, low, nt) + dot(ones, rest, nt))


def call(body, outs, spaces, scratch=(), cost=(0, 0)):
    whole = {"v": pl.BlockSpec(memory_space=pltpu.VMEM), "s": pl.BlockSpec(memory_space=pltpu.SMEM), "a": pl.BlockSpec(memory_space=pl.ANY)}
    return pl.pallas_call(
        body,
        out_shape=[jax.ShapeDtypeStruct(shape, F32) for shape in outs],
        in_specs=[whole[space] for space in spaces],
        out_specs=[whole["v"] for _ in outs],
        scratch_shapes=list(scratch),
        compiler_params=pltpu.CompilerParams(vmem_limit_bytes=VMEM_LIMIT),
        cost_estimate=pl.CostEstimate(flops=cost[0], bytes_accessed=cost[1], transcendentals=0),
    )


def on_device(sizes, features, target, out_weight, rotation, blocks, wedge):
    fwd_x, fwd_z, inv_z, inv_x = tables()
    slab = tuple(name for name, _ in PARTS["slab"])
    place = lax.axis_index(slab).astype(jnp.int32).reshape(1)
    features = features.reshape(C * ROWS, N)
    target = target.reshape(ROWS, N)
    lines, factors = call(
        forward_x,
        [(128, 128), (N, 128)],
        "ssssvavvv",
        [pltpu.VMEM((C * ROWS, N), BF16), pltpu.SemaphoreType.DMA((CHUNKS,))],
        (200_000_000, 3_000_000),
    )(place, rotation, out_weight, blocks, wedge, features, target, *fwd_x)
    lines = lax.all_to_all(lines.reshape(SLABS, 4, 128), slab, 0, 0, tiled=True).reshape(128, 128)
    (back,) = call(filter_z, [(128, 128)], "svvvvvv", (), (200_000_000, 2_000_000))(place, lines, factors, *fwd_z, *inv_z)
    back = lax.all_to_all(back.reshape(SLABS, 4, 128), slab, 0, 0, tiled=True).reshape(128, 128)
    far = math.prod(sizes[name] for name in FAR)
    near = math.prod(sizes[name] for name in NEAR)
    volume, sums = call(
        inverse_x,
        [(ROWS, N), (far, 128)],
        "vvvv",
        [pltpu.VMEM((C * YP, 128), F32)],
        (200_000_000, 3_000_000),
    )(back, features, *inv_x)
    sums = lax.all_to_all(sums.reshape(far, 1, 128), FAR, 0, 0, tiled=True)
    sums = jnp.sum(sums, 0, keepdims=True)
    sums = jnp.broadcast_to(sums, (near, 1, 128))
    sums = lax.all_to_all(sums, NEAR, 0, 0, tiled=True)
    w_grad = jnp.sum(sums, (0, 1))[:C] * (1.0 / (math.prod(sizes.values()) * ROWS * N))
    return volume.reshape(1, ZL, YP, N), w_grad


def solution(mesh):
    parts = PARTS["dp"] + PARTS["slab"]
    sizes = dict(parts)
    dp = tuple(name for name, _ in PARTS["dp"])
    slab = tuple(name for name, _ in PARTS["slab"])
    fine = Mesh(mesh.devices.reshape([size for _, size in parts]), tuple(sizes))
    in_specs = (P(dp, None, slab, None, None), P(dp, slab, None, None), P(), P(dp), P(), P())
    out_specs = (P(dp, slab, None, None), P())
    return jax.shard_map(
        functools.partial(on_device, sizes), mesh=fine, in_specs=in_specs, out_specs=out_specs, check_vma=False
    )
```

```python
import functools
import math

import jax
import jax.numpy as jnp
import numpy as np
from jax import lax
from jax.experimental import pallas as pl
from jax.experimental.pallas import tpu as pltpu
from jax.sharding import Mesh
from jax.sharding import PartitionSpec as P

N = 256
C = 64
BLK = 64
NB = 8
SLABS = 32
ZL = 8
YP = 8
ROWS = ZL * YP
CHUNKS = 4
PARTS = {"dp": (("y", 4), ("xh", 2), ("core", 2)), "slab": (("z", 16), ("xl", 2))}
NEAR = ("y", "xh")
FAR = ("core", "z", "xl")

F32, BF16 = jnp.float32, jnp.bfloat16
VMEM_LIMIT = 16 * 1024 * 1024


def halves(table):
    high = table.astype(np.float32).astype(BF16)
    low = (table - high.astype(np.float64)).astype(np.float32).astype(BF16)
    return high, low


def tables():
    step = 2.0 * math.pi / N
    space = np.arange(N)
    quad, slab = np.meshgrid(np.arange(4), np.arange(SLABS), indexing="ij")
    freq = (4 * slab + quad).reshape(-1)
    phase = (freq[:, None] * space[None, :]) % N * step
    real, imag = np.cos(phase), -np.sin(phase)
    imag[freq == 0] = np.cos(math.pi * space)
    zp, m, i = np.meshgrid(np.arange(2), np.arange(4), np.arange(SLABS), indexing="ij")
    depth = (8 * i + 2 * m + zp).reshape(-1)
    phase = (depth[:, None] * depth[None, :]) % N * step
    along = np.concatenate([np.cos(phase), np.sin(phase)], 0)
    return halves(np.concatenate([real, imag], 0)) + halves(along)


def split(values):
    high = values.astype(BF16)
    return high, (values - high.astype(F32)).astype(BF16)


def dot(left, right, dims=((1,), (0,))):
    return lax.dot_general(left, right, (dims, ((), ())), preferred_element_type=F32)


def lane_of(shape):
    return lax.broadcasted_iota(jnp.int32, shape, 1)


def regroup(pieces, to):
    group = (lane_of(pieces[0].shape) >> 4) & 3
    result = None
    for source in range(4):
        moved = pieces[source] if source == to else pltpu.roll(pieces[source], (16 * (source - to)) % 128, 1)
        result = moved if result is None else jnp.where(group == source, moved, result)
    return result


def filter_weights(turn, place, blocks, wedge, out):
    kz = lax.broadcasted_iota(jnp.int32, (8, N), 0)
    kx = lane_of((8, N)) >> 6
    listed = jnp.zeros((8, N), jnp.bool_)
    for n in range(NB):
        listed = listed | ((kz == blocks[0, n]) & (kx == blocks[1, n]))
    listed = listed.astype(F32)
    mask = jnp.concatenate(
        [wedge[a * BLK : (a + 1) * BLK, :].astype(F32) * listed[a : a + 1, :] for a in range(N // BLK)], 0
    ).astype(BF16)
    lane = lane_of((N, 128))
    row = lax.broadcasted_iota(jnp.int32, (N, 128), 0)
    quad = (lane >> 4) & 3
    freq = 4 * place + quad
    freq = jnp.where((freq == 0) & (lane >= 64), N // 2, freq)
    plus = (row == freq).astype(F32).astype(BF16)
    minus = (row == ((N - freq) & (N - 1))).astype(F32).astype(BF16)
    picks = jnp.concatenate([plus, minus], 1)
    odd = (turn & 1) == 1
    plain = dot(mask, picks)
    other = dot(mask, picks, ((0,), (0,)))
    direct = jnp.where(odd, other[:, 128:], plain[:, :128])
    mirror = jnp.where(odd, other[:, :128], plain[:, 128:]).astype(BF16)
    r = lax.broadcasted_iota(jnp.int32, (N, N), 0)
    p = 8 * (r & 31) + 2 * ((r >> 5) & 3) + (r >> 7)
    k = lane_of((N, N))
    keep = (k == p).astype(F32).astype(BF16)
    flip = (((p + k) & (N - 1)) == 0).astype(F32).astype(BF16)
    out[...] = dot(keep, direct.astype(BF16)) + dot(flip, mirror)


def forward_x(
    place, turn, weight_hbm, blocks_hbm, wedge_hbm, features_hbm, target_hbm, *refs
):
    tables_hbm, (lines, factors, features), held = refs[:4], refs[4:7], refs[7:11]
    weight, blocks, wedge, target, sems = refs[11:]
    part = C * ROWS // CHUNKS
    pairs = [(weight_hbm, weight), (blocks_hbm, blocks), (wedge_hbm, wedge), (target_hbm, target)]
    for k in range(CHUNKS):
        rows = pl.ds(k * part, part)
        pairs.append((features_hbm.at[rows], features.at[rows]))
    pairs += list(zip(tables_hbm, held))
    copies = [pltpu.make_async_copy(source, goal, sems.at[n]) for n, (source, goal) in enumerate(pairs)]
    for copy in copies:
        copy.start()
    for copy in copies[1:3]:
        copy.wait()
    filter_weights(turn[0], place[0], blocks, wedge, factors)
    copies[0].wait()
    copies[3].wait()
    total = -target[...].astype(F32)
    for k in range(CHUNKS):
        copies[4 + k].wait()
        for c in range(k * C // CHUNKS, (k + 1) * C // CHUNKS):
            total = total + weight[c] * features[c * ROWS : (c + 1) * ROWS, :].astype(F32)
    high, low = split(total)
    high = jnp.concatenate([high, high], 0)
    low = jnp.concatenate([low, low], 0)
    nt = ((1,), (1,))
    for copy in copies[4 + CHUNKS :]:
        copy.wait()
    fwd_high, fwd_low = held[:2]
    line = dot(fwd_high[...], high, nt) + (dot(fwd_high[...], low, nt) + dot(fwd_low[...], high, nt))
    line = jnp.where(lane_of((128, 128)) < 64, line[:128], line[128:])
    pieces = [line[q * SLABS : (q + 1) * SLABS] for q in range(4)]
    for m in range(4):
        lines[pl.ds(m, SLABS, stride=4), :] = regroup(pieces, m)


def filter_z(place, lines, factors, along_high, along_low, back):
    even = jnp.concatenate([lines[pl.ds(m, SLABS, stride=4), :] for m in range(4)], 0)
    data = jnp.concatenate([even, pltpu.roll(even, 120, 1)], 0)
    high, low = split(data)
    freq = dot(along_high[...], high) + (dot(along_high[...], low) + dot(along_low[...], high))
    cosine, sine = freq[:N], freq[N:]
    lane = lane_of((N, 128))
    sign = jnp.where(lane < 64, 1.0, -1.0)
    sign = jnp.where((place[0] == 0) & (((lane >> 4) & 3) == 0), 0.0, sign)
    scale = factors[...]
    kept_cosine = scale * (cosine + sign * pltpu.roll(sine, 64, 1))
    kept_sine = scale * (sine - sign * pltpu.roll(cosine, 64, 1))
    depth = None
    for kept, rows in ((kept_cosine, slice(0, N)), (kept_sine, slice(N, 2 * N))):
        high, low = split(kept)
        term = dot(along_high[rows, :], high) + (dot(along_high[rows, :], low) + dot(along_low[rows, :], high))
        depth = term if depth is None else depth + term
    lane = lane_of((SLABS, 128))
    for m in range(4):
        first = depth[m * SLABS : (m + 1) * SLABS]
        second = depth[128 + m * SLABS : 128 + (m + 1) * SLABS]
        back[pl.ds(m, SLABS, stride=4), :] = jnp.where((lane & 8) == 0, first, pltpu.roll(second, 8, 1))


def inverse_x(lines, features, fwd_high, fwd_low, volume, sums, result, partial, sem):
    blocks = [lines[pl.ds(m, SLABS, stride=4), :] for m in range(4)]
    line = jnp.concatenate([regroup(blocks, q) for q in range(4)], 0).T
    line = jnp.concatenate([line[:64], line[64:]], 1)
    line = line * jnp.where((lane_of((ROWS, N)) & 127) == 0, 1.0 / (N * N), 2.0 / (N * N))
    high, low = split(line)
    values = dot(high, fwd_high[...]) + (dot(low, fwd_high[...]) + dot(high, fwd_low[...]))
    result[...] = values
    leave = pltpu.make_async_copy(result, volume, sem)
    leave.start()

    def channels(step, carry):
        for k in range(8):
            c = step * 8 + k
            piece = features[pl.ds(pl.multiple_of(c * ROWS, ROWS), ROWS), :].astype(F32) * values
            piece = sum(piece[z * YP : (z + 1) * YP] for z in range(ZL))
            partial[pl.ds(pl.multiple_of(c * YP, YP), YP), :] = piece[:, :128] + piece[:, 128:]
        return carry

    lax.fori_loop(0, C // 8, channels, 0)
    total = sum(partial[pl.ds(y, C, stride=YP), :] for y in range(YP))
    total = jnp.concatenate([total, jnp.zeros((128 - C, 128), F32)], 0)
    high, low = split(total)
    rest = (total - high.astype(F32) - low.astype(F32)).astype(BF16)
    ones = jnp.ones((sums.shape[0], 128), BF16)
    nt = ((1,), (1,))
    sums[...] = dot(ones, high, nt) + (dot(ones, low, nt) + dot(ones, rest, nt))
    leave.wait()


def call(body, outs, spaces, scratch=(), cost=(0, 0)):
    whole = {"v": pl.BlockSpec(memory_space=pltpu.VMEM), "s": pl.BlockSpec(memory_space=pltpu.SMEM), "h": pl.BlockSpec(memory_space=pltpu.HBM)}
    ins, goals = spaces.split(">")
    return pl.pallas_call(
        body,
        out_shape=[jax.ShapeDtypeStruct(shape, kind) for shape, kind in outs],
        in_specs=[whole[space] for space in ins],
        out_specs=[whole[space] for space in goals],
        scratch_shapes=list(scratch),
        compiler_params=pltpu.CompilerParams(vmem_limit_bytes=VMEM_LIMIT),
        cost_estimate=pl.CostEstimate(flops=cost[0], bytes_accessed=cost[1], transcendentals=0),
    )


def on_device(sizes, features, target, out_weight, rotation, blocks, wedge):
    slab = tuple(name for name, _ in PARTS["slab"])
    place = lax.axis_index(slab).astype(jnp.int32).reshape(1)
    features = features.reshape(C * ROWS, N)
    target = target.reshape(ROWS, N)
    inputs = [
        pltpu.with_memory_space_constraint(jnp.asarray(each), pltpu.HBM)
        for each in (out_weight, blocks.T, wedge, features, target) + tables()
    ]
    lines, factors, features, fwd_high, fwd_low, along_high, along_low = call(
        forward_x,
        [((128, 128), F32), ((N, 128), F32), ((C * ROWS, N), BF16)] + [(table.shape, BF16) for table in inputs[5:]],
        "ss" + "h" * 9 + ">" + "v" * 7,
        [
            pltpu.SMEM((C,), F32),
            pltpu.SMEM((2, NB), jnp.int32),
            pltpu.VMEM((N, N), jnp.int32),
            pltpu.VMEM((ROWS, N), BF16),
            pltpu.SemaphoreType.DMA((8 + CHUNKS,)),
        ],
        (200_000_000, 3_000_000),
    )(place, rotation, *inputs)
    lines = lax.all_to_all(lines.reshape(SLABS, 4, 128), slab, 0, 0, tiled=True).reshape(128, 128)
    (back,) = call(filter_z, [((128, 128), F32)], "svvvv>v", (), (200_000_000, 2_000_000))(
        place, lines, factors, along_high, along_low
    )
    back = lax.all_to_all(back.reshape(SLABS, 4, 128), slab, 0, 0, tiled=True).reshape(128, 128)
    far = math.prod(sizes[name] for name in FAR)
    near = math.prod(sizes[name] for name in NEAR)
    volume, sums = call(
        inverse_x,
        [((ROWS, N), F32), ((far, 128), F32)],
        "vvvv>hv",
        [pltpu.VMEM((ROWS, N), F32), pltpu.VMEM((C * YP, 128), F32), pltpu.SemaphoreType.DMA],
        (200_000_000, 3_000_000),
    )(back, features, fwd_high, fwd_low)
    sums = lax.all_to_all(sums.reshape(far, 1, 128), FAR, 0, 0, tiled=True)
    sums = jnp.sum(sums, 0, keepdims=True)
    sums = jnp.broadcast_to(sums, (near, 1, 128))
    sums = lax.all_to_all(sums, NEAR, 0, 0, tiled=True)
    w_grad = jnp.sum(sums, (0, 1))[:C] * (1.0 / (math.prod(sizes.values()) * ROWS * N))
    return volume.reshape(1, ZL, YP, N), w_grad


def solution(mesh):
    parts = PARTS["dp"] + PARTS["slab"]
    sizes = dict(parts)
    dp = tuple(name for name, _ in PARTS["dp"])
    slab = tuple(name for name, _ in PARTS["slab"])
    fine = Mesh(mesh.devices.reshape([size for _, size in parts]), tuple(sizes))
    in_specs = (P(dp, None, slab, None, None), P(dp, slab, None, None), P(), P(dp), P(), P())
    out_specs = (P(dp, slab, None, None), P())
    return jax.shard_map(
        functools.partial(on_device, sizes), mesh=fine, in_specs=in_specs, out_specs=out_specs, check_vma=False
    )
```

```python
import functools
import math

import jax
import jax.numpy as jnp
import numpy as np
from jax import lax
from jax.experimental import pallas as pl
from jax.experimental.pallas import tpu as pltpu
from jax.sharding import Mesh
from jax.sharding import PartitionSpec as P

N = 256
C = 64
BLK = 64
NB = 8
SLABS = 32
ZL = 8
YP = 8
ROWS = ZL * YP
CHUNKS = 4
PARTS = {"dp": (("y", 4), ("xh", 2), ("core", 2)), "slab": (("z", 16), ("xl", 2))}
NEAR = ("y", "xh")
FAR = ("core", "z", "xl")

F32, BF16 = jnp.float32, jnp.bfloat16
VMEM_LIMIT = 16 * 1024 * 1024


def halves(table):
    high = table.astype(np.float32).astype(BF16)
    low = (table - high.astype(np.float64)).astype(np.float32).astype(BF16)
    return high, low


def tables():
    step = 2.0 * math.pi / N
    space = np.arange(N)
    quad, slab = np.meshgrid(np.arange(4), np.arange(SLABS), indexing="ij")
    freq = (4 * slab + quad).reshape(-1)
    phase = (freq[:, None] * space[None, :]) % N * step
    real, imag = np.cos(phase), -np.sin(phase)
    imag[freq == 0] = np.cos(math.pi * space)
    zp, m, i = np.meshgrid(np.arange(2), np.arange(4), np.arange(SLABS), indexing="ij")
    depth = (8 * i + 2 * m + zp).reshape(-1)
    phase = (depth[:, None] * depth[None, :]) % N * step
    along = np.concatenate([np.cos(phase), np.sin(phase)], 0)
    return halves(np.concatenate([real, imag], 0)) + halves(along)


def split(values):
    high = values.astype(BF16)
    return high, (values - high.astype(F32)).astype(BF16)


def dot(left, right, dims=((1,), (0,))):
    return lax.dot_general(left, right, (dims, ((), ())), preferred_element_type=F32)


def lane_of(shape):
    return lax.broadcasted_iota(jnp.int32, shape, 1)


def regroup(pieces, to):
    group = (lane_of(pieces[0].shape) >> 4) & 3
    result = None
    for source in range(4):
        moved = pieces[source] if source == to else pltpu.roll(pieces[source], (16 * (source - to)) % 128, 1)
        result = moved if result is None else jnp.where(group == source, moved, result)
    return result


def slab_index():
    return lax.axis_index(tuple(name for name, _ in PARTS["slab"])).astype(jnp.int32)


def filter_weights(turn, place, blocks, wedge, out):
    kz = lax.broadcasted_iota(jnp.int32, (8, N), 0)
    kx = lane_of((8, N)) >> 6
    listed = jnp.zeros((8, N), jnp.bool_)
    for n in range(NB):
        listed = listed | ((kz == blocks[0, n]) & (kx == blocks[1, n]))
    listed = listed.astype(F32)
    mask = jnp.concatenate(
        [wedge[a * BLK : (a + 1) * BLK, :].astype(F32) * listed[a : a + 1, :] for a in range(N // BLK)], 0
    ).astype(BF16)
    lane = lane_of((N, 128))
    row = lax.broadcasted_iota(jnp.int32, (N, 128), 0)
    quad = (lane >> 4) & 3
    freq = 4 * place + quad
    freq = jnp.where((freq == 0) & (lane >= 64), N // 2, freq)
    plus = (row == freq).astype(F32).astype(BF16)
    minus = (row == ((N - freq) & (N - 1))).astype(F32).astype(BF16)
    picks = jnp.concatenate([plus, minus], 1)
    odd = (turn & 1) == 1
    plain = dot(mask, picks)
    other = dot(mask, picks, ((0,), (0,)))
    direct = jnp.where(odd, other[:, 128:], plain[:, :128])
    mirror = jnp.where(odd, other[:, :128], plain[:, 128:]).astype(BF16)
    r = lax.broadcasted_iota(jnp.int32, (N, N), 0)
    p = 8 * (r & 31) + 2 * ((r >> 5) & 3) + (r >> 7)
    k = lane_of((N, N))
    keep = (k == p).astype(F32).astype(BF16)
    flip = (((p + k) & (N - 1)) == 0).astype(F32).astype(BF16)
    out[...] = dot(keep, direct.astype(BF16)) + dot(flip, mirror)


def forward_x(
    turn, weight_hbm, blocks_hbm, wedge_hbm, features_hbm, target_hbm, *refs
):
    tables_hbm, (lines, factors, features), held = refs[:4], refs[4:7], refs[7:11]
    weight, blocks, wedge, target, sems = refs[11:]
    part = C * ROWS // CHUNKS
    small = [(blocks_hbm, blocks), (wedge_hbm, wedge), (weight_hbm, weight), (target_hbm, target)]
    pairs = list(small)
    for k in range(CHUNKS):
        rows = pl.ds(k * part, part)
        pairs.append((features_hbm.at[rows], features.at[rows]))
    pairs += list(zip(tables_hbm, held))
    copies = [pltpu.make_async_copy(source, goal, sems.at[n]) for n, (source, goal) in enumerate(pairs)]
    for copy in copies:
        copy.start()
    for copy in copies[:2]:
        copy.wait()
    filter_weights(turn[0], slab_index(), blocks, wedge, factors)
    for copy in copies[2 : len(small)]:
        copy.wait()
    total = -target[...].astype(F32)
    for k in range(CHUNKS):
        copies[len(small) + k].wait()
        for c in range(k * C // CHUNKS, (k + 1) * C // CHUNKS):
            total = total + weight[c] * features[c * ROWS : (c + 1) * ROWS, :].astype(F32)
    high, low = split(total)
    high = jnp.concatenate([high, high], 0)
    low = jnp.concatenate([low, low], 0)
    nt = ((1,), (1,))
    for copy in copies[len(small) + CHUNKS :]:
        copy.wait()
    fwd_high, fwd_low = held[:2]
    line = dot(fwd_high[...], high, nt) + (dot(fwd_high[...], low, nt) + dot(fwd_low[...], high, nt))
    line = jnp.where(lane_of((128, 128)) < 64, line[:128], line[128:])
    pieces = [line[q * SLABS : (q + 1) * SLABS] for q in range(4)]
    for m in range(4):
        lines[pl.ds(m, SLABS, stride=4), :] = regroup(pieces, m)


def filter_z(lines, factors, along_high, along_low, back):
    even = jnp.concatenate([lines[pl.ds(m, SLABS, stride=4), :] for m in range(4)], 0)
    data = jnp.concatenate([even, pltpu.roll(even, 120, 1)], 0)
    high, low = split(data)
    freq = dot(along_high[...], high) + (dot(along_high[...], low) + dot(along_low[...], high))
    cosine, sine = freq[:N], freq[N:]
    lane = lane_of((N, 128))
    sign = jnp.where(lane < 64, 1.0, -1.0)
    sign = jnp.where((slab_index() == 0) & (((lane >> 4) & 3) == 0), 0.0, sign)
    scale = factors[...]
    kept_cosine = scale * (cosine + sign * pltpu.roll(sine, 64, 1))
    kept_sine = scale * (sine - sign * pltpu.roll(cosine, 64, 1))
    depth = None
    for kept, rows in ((kept_cosine, slice(0, N)), (kept_sine, slice(N, 2 * N))):
        high, low = split(kept)
        term = dot(along_high[rows, :], high) + (dot(along_high[rows, :], low) + dot(along_low[rows, :], high))
        depth = term if depth is None else depth + term
    lane = lane_of((SLABS, 128))
    for m in range(4):
        first = depth[m * SLABS : (m + 1) * SLABS]
        second = depth[128 + m * SLABS : 128 + (m + 1) * SLABS]
        back[pl.ds(m, SLABS, stride=4), :] = jnp.where((lane & 8) == 0, first, pltpu.roll(second, 8, 1))


def inverse_x(lines, features, fwd_high, fwd_low, volume, sums, result, partial, sem):
    blocks = [lines[pl.ds(m, SLABS, stride=4), :] for m in range(4)]
    line = jnp.concatenate([regroup(blocks, q) for q in range(4)], 0).T
    line = jnp.concatenate([line[:64], line[64:]], 1)
    line = line * jnp.where((lane_of((ROWS, N)) & 127) == 0, 1.0 / (N * N), 2.0 / (N * N))
    high, low = split(line)
    values = dot(high, fwd_high[...]) + (dot(low, fwd_high[...]) + dot(high, fwd_low[...]))
    result[...] = values
    leave = pltpu.make_async_copy(result, volume, sem)
    leave.start()

    def channels(step, carry):
        for k in range(8):
            c = step * 8 + k
            piece = features[pl.ds(pl.multiple_of(c * ROWS, ROWS), ROWS), :].astype(F32) * values
            piece = sum(piece[z * YP : (z + 1) * YP] for z in range(ZL))
            partial[pl.ds(pl.multiple_of(c * YP, YP), YP), :] = piece[:, :128] + piece[:, 128:]
        return carry

    lax.fori_loop(0, C // 8, channels, 0)
    total = sum(partial[pl.ds(y, C, stride=YP), :] for y in range(YP))
    total = jnp.concatenate([total, jnp.zeros((128 - C, 128), F32)], 0)
    high, low = split(total)
    rest = (total - high.astype(F32) - low.astype(F32)).astype(BF16)
    ones = jnp.ones((sums.shape[0], 128), BF16)
    nt = ((1,), (1,))
    sums[...] = dot(ones, high, nt) + (dot(ones, low, nt) + dot(ones, rest, nt))
    leave.wait()


def call(body, outs, spaces, scratch=(), cost=(0, 0)):
    whole = {"v": pl.BlockSpec(memory_space=pltpu.VMEM), "s": pl.BlockSpec(memory_space=pltpu.SMEM), "h": pl.BlockSpec(memory_space=pltpu.HBM)}
    ins, goals = spaces.split(">")
    return pl.pallas_call(
        body,
        out_shape=[jax.ShapeDtypeStruct(shape, kind) for shape, kind in outs],
        in_specs=[whole[space] for space in ins],
        out_specs=[whole[space] for space in goals],
        scratch_shapes=list(scratch),
        compiler_params=pltpu.CompilerParams(vmem_limit_bytes=VMEM_LIMIT),
        cost_estimate=pl.CostEstimate(flops=cost[0], bytes_accessed=cost[1], transcendentals=0),
    )


def on_device(sizes, features, target, out_weight, rotation, blocks, wedge):
    slab = tuple(name for name, _ in PARTS["slab"])
    features = features.reshape(C * ROWS, N)
    target = target.reshape(ROWS, N)
    inputs = [
        pltpu.with_memory_space_constraint(jnp.asarray(each), pltpu.HBM)
        for each in (out_weight, blocks.T, wedge, features, target) + tables()
    ]
    lines, factors, features, fwd_high, fwd_low, along_high, along_low = call(
        forward_x,
        [((128, 128), F32), ((N, 128), F32), ((C * ROWS, N), BF16)] + [(table.shape, BF16) for table in inputs[5:]],
        "s" + "h" * 9 + ">" + "v" * 7,
        [
            pltpu.SMEM((C,), F32),
            pltpu.SMEM((2, NB), jnp.int32),
            pltpu.VMEM((N, N), jnp.int32),
            pltpu.VMEM((ROWS, N), BF16),
            pltpu.SemaphoreType.DMA((8 + CHUNKS,)),
        ],
        (200_000_000, 3_000_000),
    )(rotation, *inputs)
    lines = lax.all_to_all(lines.reshape(SLABS, 4, 128), slab, 0, 0, tiled=True).reshape(128, 128)
    (back,) = call(filter_z, [((128, 128), F32)], "vvvv>v", (), (200_000_000, 2_000_000))(
        lines, factors, along_high, along_low
    )
    back = lax.all_to_all(back.reshape(SLABS, 4, 128), slab, 0, 0, tiled=True).reshape(128, 128)
    far = math.prod(sizes[name] for name in FAR)
    near = math.prod(sizes[name] for name in NEAR)
    volume, sums = call(
        inverse_x,
        [((ROWS, N), F32), ((far, 128), F32)],
        "vvvv>hv",
        [pltpu.VMEM((ROWS, N), F32), pltpu.VMEM((C * YP, 128), F32), pltpu.SemaphoreType.DMA],
        (200_000_000, 3_000_000),
    )(back, features, fwd_high, fwd_low)
    sums = lax.all_to_all(sums.reshape(far, 1, 128), FAR, 0, 0, tiled=True)
    sums = jnp.sum(sums, 0, keepdims=True)
    sums = jnp.broadcast_to(sums, (near, 1, 128))
    sums = lax.all_to_all(sums, NEAR, 0, 0, tiled=True)
    w_grad = jnp.sum(sums, (0, 1))[:C] * (1.0 / (math.prod(sizes.values()) * ROWS * N))
    return volume.reshape(1, ZL, YP, N), w_grad


def solution(mesh):
    parts = PARTS["dp"] + PARTS["slab"]
    sizes = dict(parts)
    dp = tuple(name for name, _ in PARTS["dp"])
    slab = tuple(name for name, _ in PARTS["slab"])
    fine = Mesh(mesh.devices.reshape([size for _, size in parts]), tuple(sizes))
    in_specs = (P(dp, None, slab, None, None), P(dp, slab, None, None), P(), P(dp), P(), P())
    out_specs = (P(dp, slab, None, None), P())
    return jax.shard_map(
        functools.partial(on_device, sizes), mesh=fine, in_specs=in_specs, out_specs=out_specs, check_vma=False
    )
```

```python
import functools
import math

import jax
import jax.numpy as jnp
import numpy as np
from jax import lax
from jax.experimental import pallas as pl
from jax.experimental.pallas import tpu as pltpu
from jax.sharding import Mesh
from jax.sharding import PartitionSpec as P

N = 256
C = 64
BLK = 64
NB = 8
SLABS = 32
ZL = 8
YP = 8
ROWS = ZL * YP
CHUNKS = 4
PARTS = {"dp": (("y", 4), ("xh", 2), ("core", 2)), "slab": (("zh", 4), ("zl", 4), ("xl", 2))}
GROUPS = 4
SETS = 4
NEAR = ("y", "xh")
FAR = ("core", "zh", "zl", "xl")
INSIDE = ("zl", "xl")

F32, BF16 = jnp.float32, jnp.bfloat16
VMEM_LIMIT = 16 * 1024 * 1024


def halves(table):
    high = table.astype(np.float32).astype(BF16)
    low = (table - high.astype(np.float64)).astype(np.float32).astype(BF16)
    return high, low


def tables():
    step = 2.0 * math.pi / N
    space = np.arange(N)
    quad, slab = np.meshgrid(np.arange(4), np.arange(SLABS), indexing="ij")
    freq = (4 * slab + quad).reshape(-1)
    phase = (freq[:, None] * space[None, :]) % N * step
    real, imag = np.cos(phase), -np.sin(phase)
    imag[freq == 0] = np.cos(math.pi * space)
    zh, zp, m, k = np.meshgrid(np.arange(GROUPS), np.arange(2), np.arange(4), np.arange(8), indexing="ij")
    depth = (64 * zh + 8 * k + 2 * m + zp).reshape(-1)
    phase = (depth[:, None] * depth[None, :]) % N * step
    along = np.concatenate([np.cos(phase), np.sin(phase)], 0)
    return halves(np.concatenate([real, imag], 0)) + halves(along)


def split(values):
    high = values.astype(BF16)
    return high, (values - high.astype(F32)).astype(BF16)


def dot(left, right, dims=((1,), (0,))):
    return lax.dot_general(left, right, (dims, ((), ())), preferred_element_type=F32)


def lane_of(shape):
    return lax.broadcasted_iota(jnp.int32, shape, 1)


def regroup(pieces, to):
    group = (lane_of(pieces[0].shape) >> 4) & 3
    result = None
    for source in range(4):
        moved = pieces[source] if source == to else pltpu.roll(pieces[source], (16 * (source - to)) % 128, 1)
        result = moved if result is None else jnp.where(group == source, moved, result)
    return result


def filter_weights(turn, blocks, wedge, out):
    kz = lax.broadcasted_iota(jnp.int32, (8, N), 0)
    kx = lane_of((8, N)) >> 6
    listed = jnp.zeros((8, N), jnp.bool_)
    for n in range(NB):
        listed = listed | ((kz == blocks[0, n]) & (kx == blocks[1, n]))
    listed = listed.astype(F32)
    mask = jnp.concatenate(
        [wedge[a * BLK : (a + 1) * BLK, :].astype(F32) * listed[a : a + 1, :] for a in range(N // BLK)], 0
    ).astype(BF16)
    lane = lane_of((N, N))
    row = lax.broadcasted_iota(jnp.int32, (N, N), 0)
    part, quad, odd_set, pair = (lane >> 6) & 1, (lane >> 4) & 3, (lane >> 3) & 1, lane >> 7
    freq = 16 * lax.axis_index(INSIDE).astype(jnp.int32) + 8 * pair + 4 * odd_set + quad
    freq = jnp.where((freq == 0) & (part == 1), N // 2, freq)
    plus = (row == freq).astype(F32).astype(BF16)
    minus = (row == ((N - freq) & (N - 1))).astype(F32).astype(BF16)
    odd = (turn & 1) == 1
    direct = jnp.where(odd, dot(mask, minus, ((0,), (0,))), dot(mask, plus)).astype(BF16)
    mirror = jnp.where(odd, dot(mask, plus, ((0,), (0,))), dot(mask, minus)).astype(BF16)
    p = (row & 192) + 8 * (row & 7) + 2 * ((row >> 3) & 3) + ((row >> 5) & 1)
    keep = (lane == p).astype(F32).astype(BF16)
    flip = (((p + lane) & (N - 1)) == 0).astype(F32).astype(BF16)
    out[...] = dot(keep, direct) + dot(flip, mirror)


def forward_x(
    turn, weight_hbm, blocks_hbm, wedge_hbm, features_hbm, target_hbm, *refs
):
    tables_hbm, (lines, factors, features), held = refs[:4], refs[4:7], refs[7:11]
    weight, blocks, wedge, target, sems = refs[11:]
    part = C * ROWS // CHUNKS
    small = [(blocks_hbm, blocks), (wedge_hbm, wedge), (weight_hbm, weight), (target_hbm, target)]
    pairs = list(small)
    for k in range(CHUNKS):
        rows = pl.ds(k * part, part)
        pairs.append((features_hbm.at[rows], features.at[rows]))
    pairs += list(zip(tables_hbm, held))
    copies = [pltpu.make_async_copy(source, goal, sems.at[n]) for n, (source, goal) in enumerate(pairs)]
    for copy in copies:
        copy.start()
    for copy in copies[:2]:
        copy.wait()
    filter_weights(turn[0], blocks, wedge, factors)
    for copy in copies[2 : len(small)]:
        copy.wait()
    total = -target[...].astype(F32)
    for k in range(CHUNKS):
        copies[len(small) + k].wait()
        for c in range(k * C // CHUNKS, (k + 1) * C // CHUNKS):
            total = total + weight[c] * features[c * ROWS : (c + 1) * ROWS, :].astype(F32)
    high, low = split(total)
    high = jnp.concatenate([high, high], 0)
    low = jnp.concatenate([low, low], 0)
    nt = ((1,), (1,))
    for copy in copies[len(small) + CHUNKS :]:
        copy.wait()
    fwd_high, fwd_low = held[:2]
    line = dot(fwd_high[...], high, nt) + (dot(fwd_high[...], low, nt) + dot(fwd_low[...], high, nt))
    line = jnp.where(lane_of((128, 128)) < 64, line[:128], line[128:])
    pieces = [line[q * SLABS : (q + 1) * SLABS] for q in range(4)]
    for m in range(4):
        moved = regroup(pieces, m)
        for zh in range(GROUPS):
            lines[pl.ds(zh * 128 + m, SLABS, stride=4), :] = moved


def filter_z(lines, factors, along_high, along_low, back):
    near = (lane_of((SLABS, 128)) & 8) == 0
    halves_of = []
    for pair in range(SETS // 2):
        rows = {}
        for m in range(4):
            first = lines[pl.ds(8 * pair + m, SLABS, stride=16), :]
            second = lines[pl.ds(8 * pair + 4 + m, SLABS, stride=16), :]
            rows[0, m] = jnp.where(near, first, pltpu.roll(second, 8, 1))
            rows[1, m] = jnp.where(near, pltpu.roll(first, 120, 1), second)
        halves_of.append(
            jnp.concatenate(
                [rows[zp, m][8 * zh : 8 * zh + 8] for zh in range(GROUPS) for zp in range(2) for m in range(4)], 0
            )
        )
    high, low = split(jnp.concatenate(halves_of, 1))
    freq = dot(along_high[...], high) + (dot(along_high[...], low) + dot(along_low[...], high))
    lane = lane_of((N, 128))
    sign = jnp.where(lane < 64, 1.0, -1.0)
    alone = (lax.axis_index(INSIDE) == 0) & ((lane & 56) == 0)
    kept = []
    for pair in range(SETS // 2):
        cosine = freq[:N, 128 * pair : 128 * pair + 128]
        sine = freq[N:, 128 * pair : 128 * pair + 128]
        mix = jnp.where(alone, 0.0, sign) if pair == 0 else sign
        scale = factors[:, 128 * pair : 128 * pair + 128]
        kept.append((scale * (cosine + mix * pltpu.roll(sine, 64, 1)), scale * (sine - mix * pltpu.roll(cosine, 64, 1))))
    own = lax.axis_index("zh") * 64
    depth = None
    for part in range(2):
        rows = pl.ds(pl.multiple_of(part * N + own, 64), 64)
        high, low = split(jnp.concatenate([pieces[part] for pieces in kept], 1))
        term = dot(along_high[rows, :], high) + (dot(along_high[rows, :], low) + dot(along_low[rows, :], high))
        depth = term if depth is None else depth + term
    near = (lane_of((8, 128)) & 8) == 0
    for pair in range(SETS // 2):
        for m in range(4):
            even = depth[8 * m : 8 * m + 8, 128 * pair : 128 * pair + 128]
            odd = depth[32 + 8 * m : 40 + 8 * m, 128 * pair : 128 * pair + 128]
            back[pl.ds(8 * pair + m, 8, stride=16), :] = jnp.where(near, even, pltpu.roll(odd, 8, 1))
            back[pl.ds(8 * pair + 4 + m, 8, stride=16), :] = jnp.where(near, pltpu.roll(even, 120, 1), odd)


def inverse_x(lines, features, fwd_high, fwd_low, volume, sums, result, partial, sem):
    blocks = [lines[pl.ds(m, SLABS, stride=4), :] for m in range(4)]
    line = jnp.concatenate([regroup(blocks, q) for q in range(4)], 0).T
    line = jnp.concatenate([line[:64], line[64:]], 1)
    line = line * jnp.where((lane_of((ROWS, N)) & 127) == 0, 1.0 / (N * N), 2.0 / (N * N))
    high, low = split(line)
    values = dot(high, fwd_high[...]) + (dot(low, fwd_high[...]) + dot(high, fwd_low[...]))
    result[...] = values
    leave = pltpu.make_async_copy(result, volume, sem)
    leave.start()

    def channels(step, carry):
        for k in range(8):
            c = step * 8 + k
            piece = features[pl.ds(pl.multiple_of(c * ROWS, ROWS), ROWS), :].astype(F32) * values
            piece = sum(piece[z * YP : (z + 1) * YP] for z in range(ZL))
            partial[pl.ds(pl.multiple_of(c * YP, YP), YP), :] = piece[:, :128] + piece[:, 128:]
        return carry

    lax.fori_loop(0, C // 8, channels, 0)
    total = sum(partial[pl.ds(y, C, stride=YP), :] for y in range(YP))
    total = jnp.concatenate([total, jnp.zeros((128 - C, 128), F32)], 0)
    high, low = split(total)
    rest = (total - high.astype(F32) - low.astype(F32)).astype(BF16)
    ones = jnp.ones((sums.shape[0], 128), BF16)
    nt = ((1,), (1,))
    sums[...] = dot(ones, high, nt) + (dot(ones, low, nt) + dot(ones, rest, nt))
    leave.wait()


def call(body, outs, spaces, scratch=(), cost=(0, 0)):
    whole = {"v": pl.BlockSpec(memory_space=pltpu.VMEM), "s": pl.BlockSpec(memory_space=pltpu.SMEM), "h": pl.BlockSpec(memory_space=pltpu.HBM)}
    ins, goals = spaces.split(">")
    return pl.pallas_call(
        body,
        out_shape=[jax.ShapeDtypeStruct(shape, kind) for shape, kind in outs],
        in_specs=[whole[space] for space in ins],
        out_specs=[whole[space] for space in goals],
        scratch_shapes=list(scratch),
        compiler_params=pltpu.CompilerParams(vmem_limit_bytes=VMEM_LIMIT),
        cost_estimate=pl.CostEstimate(flops=cost[0], bytes_accessed=cost[1], transcendentals=0),
    )


def on_device(sizes, features, target, out_weight, rotation, blocks, wedge):
    slab = tuple(name for name, _ in PARTS["slab"])
    features = features.reshape(C * ROWS, N)
    target = target.reshape(ROWS, N)
    inputs = [
        pltpu.with_memory_space_constraint(jnp.asarray(each), pltpu.HBM)
        for each in (out_weight, blocks.T, wedge, features, target) + tables()
    ]
    lines, factors, features, fwd_high, fwd_low, along_high, along_low = call(
        forward_x,
        [((GROUPS * 128, 128), F32), ((N, N), F32), ((C * ROWS, N), BF16)] + [(table.shape, BF16) for table in inputs[5:]],
        "s" + "h" * 9 + ">" + "v" * 7,
        [
            pltpu.SMEM((C,), F32),
            pltpu.SMEM((2, NB), jnp.int32),
            pltpu.VMEM((N, N), jnp.int32),
            pltpu.VMEM((ROWS, N), BF16),
            pltpu.SemaphoreType.DMA((8 + CHUNKS,)),
        ],
        (200_000_000, 3_000_000),
    )(rotation, *inputs)
    lines = lax.all_to_all(lines.reshape(SLABS, 16, 128), slab, 0, 0, tiled=True).reshape(SLABS * 16, 128)
    (back,) = call(filter_z, [((128, 128), F32)], "vvvv>v", (), (200_000_000, 2_000_000))(
        lines, factors, along_high, along_low
    )
    back = lax.all_to_all(back.reshape(8, 16, 128), INSIDE, 0, 0, tiled=True).reshape(128, 128)
    far = math.prod(sizes[name] for name in FAR)
    near = math.prod(sizes[name] for name in NEAR)
    volume, sums = call(
        inverse_x,
        [((ROWS, N), F32), ((far, 128), F32)],
        "vvvv>hv",
        [pltpu.VMEM((ROWS, N), F32), pltpu.VMEM((C * YP, 128), F32), pltpu.SemaphoreType.DMA],
        (200_000_000, 3_000_000),
    )(back, features, fwd_high, fwd_low)
    sums = lax.all_to_all(sums.reshape(far, 1, 128), FAR, 0, 0, tiled=True)
    sums = jnp.sum(sums, 0, keepdims=True)
    sums = jnp.broadcast_to(sums, (near, 1, 128))
    sums = lax.all_to_all(sums, NEAR, 0, 0, tiled=True)
    w_grad = jnp.sum(sums, (0, 1))[:C] * (1.0 / (math.prod(sizes.values()) * ROWS * N))
    return volume.reshape(1, ZL, YP, N), w_grad


def solution(mesh):
    parts = PARTS["dp"] + PARTS["slab"]
    sizes = dict(parts)
    dp = tuple(name for name, _ in PARTS["dp"])
    slab = tuple(name for name, _ in PARTS["slab"])
    fine = Mesh(mesh.devices.reshape([size for _, size in parts]), tuple(sizes))
    in_specs = (P(dp, None, slab, None, None), P(dp, slab, None, None), P(), P(dp), P(), P())
    out_specs = (P(dp, slab, None, None), P())
    return jax.shard_map(
        functools.partial(on_device, sizes), mesh=fine, in_specs=in_specs, out_specs=out_specs, check_vma=False
    )
```

```python
import functools
import math

import jax
import jax.numpy as jnp
import numpy as np
from jax import lax
from jax.experimental import pallas as pl
from jax.experimental.pallas import tpu as pltpu
from jax.sharding import Mesh
from jax.sharding import PartitionSpec as P

N = 256
C = 64
BLK = 64
NB = 8
SLABS = 32
ZL = 8
YP = 8
ROWS = ZL * YP
CHUNKS = 8
PARTS = {"dp": (("y", 4), ("xh", 2), ("core", 2)), "slab": (("z", 16), ("xl", 2))}
NEAR = ("y", "xh")
FAR = ("core", "z", "xl")

F32, BF16 = jnp.float32, jnp.bfloat16
VMEM_LIMIT = 16 * 1024 * 1024


def halves(table):
    high = table.astype(np.float32).astype(BF16)
    low = (table - high.astype(np.float64)).astype(np.float32).astype(BF16)
    return high, low


def tables():
    step = 2.0 * math.pi / N
    space = np.arange(N)
    quad, slab = np.meshgrid(np.arange(4), np.arange(SLABS), indexing="ij")
    freq = (4 * slab + quad).reshape(-1)
    phase = (freq[:, None] * space[None, :]) % N * step
    real, imag = np.cos(phase), -np.sin(phase)
    imag[freq == 0] = np.cos(math.pi * space)
    zp, m, i = np.meshgrid(np.arange(2), np.arange(4), np.arange(SLABS), indexing="ij")
    depth = (8 * i + 2 * m + zp).reshape(-1)
    phase = (depth[:, None] * depth[None, :]) % N * step
    along = np.concatenate([np.cos(phase), np.sin(phase)], 0)
    return halves(np.concatenate([real, imag], 0)) + halves(along)


def split(values):
    high = values.astype(BF16)
    return high, (values - high.astype(F32)).astype(BF16)


def dot(left, right, dims=((1,), (0,))):
    return lax.dot_general(left, right, (dims, ((), ())), preferred_element_type=F32)


def lane_of(shape):
    return lax.broadcasted_iota(jnp.int32, shape, 1)


def regroup(pieces, to):
    group = (lane_of(pieces[0].shape) >> 4) & 3
    result = None
    for source in range(4):
        moved = pieces[source] if source == to else pltpu.roll(pieces[source], (16 * (source - to)) % 128, 1)
        result = moved if result is None else jnp.where(group == source, moved, result)
    return result


def slab_index():
    return lax.axis_index(tuple(name for name, _ in PARTS["slab"])).astype(jnp.int32)


def filter_weights(turn, place, blocks, wedge, out):
    kz = lax.broadcasted_iota(jnp.int32, (8, N), 0)
    kx = lane_of((8, N)) >> 6
    listed = jnp.zeros((8, N), jnp.bool_)
    for n in range(NB):
        listed = listed | ((kz == blocks[0, n]) & (kx == blocks[1, n]))
    listed = listed.astype(F32)
    mask = jnp.concatenate(
        [wedge[a * BLK : (a + 1) * BLK, :].astype(F32) * listed[a : a + 1, :] for a in range(N // BLK)], 0
    ).astype(BF16)
    lane = lane_of((N, 128))
    row = lax.broadcasted_iota(jnp.int32, (N, 128), 0)
    quad = (lane >> 4) & 3
    freq = 4 * place + quad
    freq = jnp.where((freq == 0) & (lane >= 64), N // 2, freq)
    plus = (row == freq).astype(F32).astype(BF16)
    minus = (row == ((N - freq) & (N - 1))).astype(F32).astype(BF16)
    picks = jnp.concatenate([plus, minus], 1)
    odd = (turn & 1) == 1
    plain = dot(mask, picks)
    other = dot(mask, picks, ((0,), (0,)))
    direct = jnp.where(odd, other[:, 128:], plain[:, :128])
    mirror = jnp.where(odd, other[:, :128], plain[:, 128:]).astype(BF16)
    r = lax.broadcasted_iota(jnp.int32, (N, N), 0)
    p = 8 * (r & 31) + 2 * ((r >> 5) & 3) + (r >> 7)
    k = lane_of((N, N))
    keep = (k == p).astype(F32).astype(BF16)
    flip = (((p + k) & (N - 1)) == 0).astype(F32).astype(BF16)
    out[...] = dot(keep, direct.astype(BF16)) + dot(flip, mirror)


def prepare(turn, blocks_hbm, wedge_hbm, high_hbm, low_hbm, factors, high, low, blocks, wedge, sems):
    pairs = [(blocks_hbm, blocks), (wedge_hbm, wedge), (high_hbm, high), (low_hbm, low)]
    copies = [pltpu.make_async_copy(source, goal, sems.at[n]) for n, (source, goal) in enumerate(pairs)]
    for copy in copies:
        copy.start()
    for copy in copies[:2]:
        copy.wait()
    filter_weights(turn[0], slab_index(), blocks, wedge, factors)
    for copy in copies[2:]:
        copy.wait()


def forward_x(weight_hbm, target_hbm, features_hbm, high_hbm, low_hbm, lines, features, fwd_high, fwd_low, weight, target, sems):
    part = C * ROWS // CHUNKS
    pairs = [(weight_hbm, weight), (target_hbm, target)]
    for k in range(CHUNKS):
        rows = pl.ds(k * part, part)
        pairs.append((features_hbm.at[rows], features.at[rows]))
    pairs += [(high_hbm, fwd_high), (low_hbm, fwd_low)]
    copies = [pltpu.make_async_copy(source, goal, sems.at[n]) for n, (source, goal) in enumerate(pairs)]
    for copy in copies:
        copy.start()
    for copy in copies[:2]:
        copy.wait()
    total = -target[...].astype(F32)
    for k in range(CHUNKS):
        copies[2 + k].wait()
        for c in range(k * C // CHUNKS, (k + 1) * C // CHUNKS):
            total = total + weight[c] * features[c * ROWS : (c + 1) * ROWS, :].astype(F32)
    high, low = split(total)
    nt = ((1,), (1,))
    for copy in copies[2 + CHUNKS :]:
        copy.wait()
    both = dot(fwd_high[...], jnp.concatenate([high, low], 0), nt)
    line = dot(fwd_low[...], jnp.concatenate([high, high], 0), nt) + (both + pltpu.roll(both, 64, 1))
    line = jnp.where(lane_of((128, 128)) < 64, line[:128], line[128:])
    pieces = [line[q * SLABS : (q + 1) * SLABS] for q in range(4)]
    for m in range(4):
        lines[pl.ds(m, SLABS, stride=4), :] = regroup(pieces, m)


def three(left_high, left_low, right):
    high, low = split(right)
    both = dot(left_high, jnp.concatenate([high, low], 1))
    return dot(left_low, high) + (both[:, :128] + both[:, 128:])


def filter_z(lines, factors, along_high, along_low, back):
    even = jnp.concatenate([lines[pl.ds(m, SLABS, stride=4), :] for m in range(4)], 0)
    data = jnp.concatenate([even, pltpu.roll(even, 120, 1)], 0)
    freq = three(along_high[...], along_low[...], data)
    cosine, sine = freq[:N], freq[N:]
    lane = lane_of((N, 128))
    sign = jnp.where(lane < 64, 1.0, -1.0)
    sign = jnp.where((slab_index() == 0) & (((lane >> 4) & 3) == 0), 0.0, sign)
    scale = factors[...]
    kept_cosine = scale * (cosine + sign * pltpu.roll(sine, 64, 1))
    kept_sine = scale * (sine - sign * pltpu.roll(cosine, 64, 1))
    depth = three(along_high[:N, :], along_low[:N, :], kept_cosine) + three(along_high[N:, :], along_low[N:, :], kept_sine)
    lane = lane_of((SLABS, 128))
    for m in range(4):
        first = depth[m * SLABS : (m + 1) * SLABS]
        second = depth[128 + m * SLABS : 128 + (m + 1) * SLABS]
        back[pl.ds(m, SLABS, stride=4), :] = jnp.where((lane & 8) == 0, first, pltpu.roll(second, 8, 1))


def inverse_x(lines, features, fwd_high, fwd_low, volume, sums, result, partial, sem):
    blocks = [lines[pl.ds(m, SLABS, stride=4), :] for m in range(4)]
    line = jnp.concatenate([regroup(blocks, q) for q in range(4)], 0).T
    line = jnp.concatenate([line[:64], line[64:]], 1)
    line = line * jnp.where((lane_of((ROWS, N)) & 127) == 0, 1.0 / (N * N), 2.0 / (N * N))
    high, low = split(line)
    both = dot(jnp.concatenate([high, low], 0), fwd_high[...])
    values = both[:ROWS] + (both[ROWS:] + dot(high, fwd_low[...]))
    result[...] = values
    leave = pltpu.make_async_copy(result, volume, sem)
    leave.start()

    def channels(step, carry):
        for k in range(8):
            c = step * 8 + k
            piece = features[pl.ds(pl.multiple_of(c * ROWS, ROWS), ROWS), :].astype(F32) * values
            piece = sum(piece[z * YP : (z + 1) * YP] for z in range(ZL))
            partial[pl.ds(pl.multiple_of(c * YP, YP), YP), :] = piece[:, :128] + piece[:, 128:]
        return carry

    lax.fori_loop(0, C // 8, channels, 0)
    total = sum(partial[pl.ds(y, C, stride=YP), :] for y in range(YP))
    total = jnp.concatenate([total, jnp.zeros((128 - C, 128), F32)], 0)
    high, low = split(total)
    rest = (total - high.astype(F32) - low.astype(F32)).astype(BF16)
    ones = jnp.ones((sums.shape[0], 128), BF16)
    nt = ((1,), (1,))
    sums[...] = dot(ones, high, nt) + (dot(ones, low, nt) + dot(ones, rest, nt))
    leave.wait()


def call(body, outs, spaces, scratch=(), cost=(0, 0)):
    whole = {"v": pl.BlockSpec(memory_space=pltpu.VMEM), "s": pl.BlockSpec(memory_space=pltpu.SMEM), "h": pl.BlockSpec(memory_space=pltpu.HBM)}
    ins, goals = spaces.split(">")
    return pl.pallas_call(
        body,
        out_shape=[jax.ShapeDtypeStruct(shape, kind) for shape, kind in outs],
        in_specs=[whole[space] for space in ins],
        out_specs=[whole[space] for space in goals],
        scratch_shapes=list(scratch),
        compiler_params=pltpu.CompilerParams(vmem_limit_bytes=VMEM_LIMIT),
        cost_estimate=pl.CostEstimate(flops=cost[0], bytes_accessed=cost[1], transcendentals=0),
    )


def hbm(array):
    return pltpu.with_memory_space_constraint(array, pltpu.HBM)


def on_device(sizes, features, target, out_weight, rotation, blocks, wedge):
    slab = tuple(name for name, _ in PARTS["slab"])
    features = features.reshape(C * ROWS, N)
    target = target.reshape(ROWS, N)
    fwd_high, fwd_low, along_high, along_low = [hbm(jnp.asarray(table)) for table in tables()]
    lines, features, fwd_high, fwd_low = call(
        forward_x,
        [((128, 128), F32), ((C * ROWS, N), BF16), (fwd_high.shape, BF16), (fwd_low.shape, BF16)],
        "hhhhh>vvvv",
        [pltpu.SMEM((C,), F32), pltpu.VMEM((ROWS, N), BF16), pltpu.SemaphoreType.DMA((4 + CHUNKS,))],
        (200_000_000, 3_000_000),
    )(hbm(out_weight), hbm(target), hbm(features), fwd_high, fwd_low)
    rotation, lines = lax.optimization_barrier((rotation, lines))
    factors, along_high, along_low = call(
        prepare,
        [((N, 128), F32), (along_high.shape, BF16), (along_low.shape, BF16)],
        "shhhh>vvv",
        [pltpu.SMEM((2, NB), jnp.int32), pltpu.VMEM((N, N), jnp.int32), pltpu.SemaphoreType.DMA((4,))],
        (200_000_000, 3_000_000),
    )(rotation, hbm(blocks.T), hbm(wedge), along_high, along_low)
    lines = lax.all_to_all(lines.reshape(SLABS, 4, 128), slab, 0, 0, tiled=True).reshape(128, 128)
    (back,) = call(filter_z, [((128, 128), F32)], "vvvv>v", (), (200_000_000, 2_000_000))(
        lines, factors, along_high, along_low
    )
    back = lax.all_to_all(back.reshape(SLABS, 4, 128), slab, 0, 0, tiled=True).reshape(128, 128)
    far = math.prod(sizes[name] for name in FAR)
    near = math.prod(sizes[name] for name in NEAR)
    volume, sums = call(
        inverse_x,
        [((ROWS, N), F32), ((far, 128), F32)],
        "vvvv>hv",
        [pltpu.VMEM((ROWS, N), F32), pltpu.VMEM((C * YP, 128), F32), pltpu.SemaphoreType.DMA],
        (200_000_000, 3_000_000),
    )(back, features, fwd_high, fwd_low)
    sums = lax.all_to_all(sums.reshape(far, 1, 128), FAR, 0, 0, tiled=True)
    sums = jnp.sum(sums, 0, keepdims=True)
    sums = jnp.broadcast_to(sums, (near, 1, 128))
    sums = lax.all_to_all(sums, NEAR, 0, 0, tiled=True)
    w_grad = jnp.sum(sums, (0, 1))[:C] * (1.0 / (math.prod(sizes.values()) * ROWS * N))
    return volume.reshape(1, ZL, YP, N), w_grad


def solution(mesh):
    parts = PARTS["dp"] + PARTS["slab"]
    sizes = dict(parts)
    dp = tuple(name for name, _ in PARTS["dp"])
    slab = tuple(name for name, _ in PARTS["slab"])
    fine = Mesh(mesh.devices.reshape([size for _, size in parts]), tuple(sizes))
    in_specs = (P(dp, None, slab, None, None), P(dp, slab, None, None), P(), P(dp), P(), P())
    out_specs = (P(dp, slab, None, None), P())
    return jax.shard_map(
        functools.partial(on_device, sizes), mesh=fine, in_specs=in_specs, out_specs=out_specs, check_vma=False
    )
```

```python
import functools
import math

import jax
import jax.numpy as jnp
import numpy as np
from jax import lax
from jax.experimental import pallas as pl
from jax.experimental.pallas import tpu as pltpu
from jax.sharding import Mesh
from jax.sharding import PartitionSpec as P

N = 256
C = 64
BLK = 64
NB = 8
SLABS = 32
ZL = 8
YP = 8
ROWS = ZL * YP
CHUNKS = 8
PARTS = {"dp": (("y", 4), ("xh", 2), ("core", 2)), "slab": (("zh", 4), ("zl", 4), ("xl", 2))}
GROUPS = 4
SETS = 4
NEAR = ("y", "xh")
FAR = ("core", "zh", "zl", "xl")
INSIDE = ("zl", "xl")

F32, BF16 = jnp.float32, jnp.bfloat16
VMEM_LIMIT = 16 * 1024 * 1024


def halves(table):
    high = table.astype(np.float32).astype(BF16)
    low = (table - high.astype(np.float64)).astype(np.float32).astype(BF16)
    return high, low


def tables():
    step = 2.0 * math.pi / N
    space = np.arange(N)
    quad, slab = np.meshgrid(np.arange(4), np.arange(SLABS), indexing="ij")
    freq = (4 * slab + quad).reshape(-1)
    phase = (freq[:, None] * space[None, :]) % N * step
    real, imag = np.cos(phase), -np.sin(phase)
    imag[freq == 0] = np.cos(math.pi * space)
    zh, zp, m, k = np.meshgrid(np.arange(GROUPS), np.arange(2), np.arange(4), np.arange(8), indexing="ij")
    depth = (64 * zh + 8 * k + 2 * m + zp).reshape(-1)
    phase = (depth[:, None] * depth[None, :]) % N * step
    along = np.concatenate([np.cos(phase), np.sin(phase)], 0)
    return halves(np.concatenate([real, imag], 0)) + halves(along)


def split(values):
    high = values.astype(BF16)
    return high, (values - high.astype(F32)).astype(BF16)


def dot(left, right, dims=((1,), (0,))):
    return lax.dot_general(left, right, (dims, ((), ())), preferred_element_type=F32)


def lane_of(shape):
    return lax.broadcasted_iota(jnp.int32, shape, 1)


def regroup(pieces, to):
    group = (lane_of(pieces[0].shape) >> 4) & 3
    result = None
    for source in range(4):
        moved = pieces[source] if source == to else pltpu.roll(pieces[source], (16 * (source - to)) % 128, 1)
        result = moved if result is None else jnp.where(group == source, moved, result)
    return result


def filter_weights(turn, blocks, wedge, out):
    kz = lax.broadcasted_iota(jnp.int32, (8, N), 0)
    kx = lane_of((8, N)) >> 6
    listed = jnp.zeros((8, N), jnp.bool_)
    for n in range(NB):
        listed = listed | ((kz == blocks[0, n]) & (kx == blocks[1, n]))
    listed = listed.astype(F32)
    mask = jnp.concatenate(
        [wedge[a * BLK : (a + 1) * BLK, :].astype(F32) * listed[a : a + 1, :] for a in range(N // BLK)], 0
    ).astype(BF16)
    lane = lane_of((N, N))
    row = lax.broadcasted_iota(jnp.int32, (N, N), 0)
    part, quad, odd_set, pair = (lane >> 6) & 1, (lane >> 4) & 3, (lane >> 3) & 1, lane >> 7
    freq = 16 * lax.axis_index(INSIDE).astype(jnp.int32) + 8 * pair + 4 * odd_set + quad
    freq = jnp.where((freq == 0) & (part == 1), N // 2, freq)
    plus = (row == freq).astype(F32).astype(BF16)
    minus = (row == ((N - freq) & (N - 1))).astype(F32).astype(BF16)
    odd = (turn & 1) == 1
    direct = jnp.where(odd, dot(mask, minus, ((0,), (0,))), dot(mask, plus)).astype(BF16)
    mirror = jnp.where(odd, dot(mask, plus, ((0,), (0,))), dot(mask, minus)).astype(BF16)
    p = (row & 192) + 8 * (row & 7) + 2 * ((row >> 3) & 3) + ((row >> 5) & 1)
    keep = (lane == p).astype(F32).astype(BF16)
    flip = (((p + lane) & (N - 1)) == 0).astype(F32).astype(BF16)
    out[...] = dot(keep, direct) + dot(flip, mirror)


def prepare(turn, blocks_hbm, wedge_hbm, high_hbm, low_hbm, factors, high, low, blocks, wedge, sems):
    pairs = [(blocks_hbm, blocks), (wedge_hbm, wedge), (high_hbm, high), (low_hbm, low)]
    copies = [pltpu.make_async_copy(source, goal, sems.at[n]) for n, (source, goal) in enumerate(pairs)]
    for copy in copies:
        copy.start()
    for copy in copies[:2]:
        copy.wait()
    filter_weights(turn[0], blocks, wedge, factors)
    for copy in copies[2:]:
        copy.wait()


def forward_x(weight_hbm, target_hbm, features_hbm, high_hbm, low_hbm, lines, features, fwd_high, fwd_low, weight, target, sems):
    part = C * ROWS // CHUNKS
    pairs = [(weight_hbm, weight), (target_hbm, target)]
    for k in range(CHUNKS):
        rows = pl.ds(k * part, part)
        pairs.append((features_hbm.at[rows], features.at[rows]))
    pairs += [(high_hbm, fwd_high), (low_hbm, fwd_low)]
    copies = [pltpu.make_async_copy(source, goal, sems.at[n]) for n, (source, goal) in enumerate(pairs)]
    for copy in copies:
        copy.start()
    for copy in copies[:2]:
        copy.wait()
    total = -target[...].astype(F32)
    for k in range(CHUNKS):
        copies[2 + k].wait()
        for c in range(k * C // CHUNKS, (k + 1) * C // CHUNKS):
            total = total + weight[c] * features[c * ROWS : (c + 1) * ROWS, :].astype(F32)
    high, low = split(total)
    nt = ((1,), (1,))
    for copy in copies[2 + CHUNKS :]:
        copy.wait()
    both = dot(fwd_high[...], jnp.concatenate([high, low], 0), nt)
    line = dot(fwd_low[...], jnp.concatenate([high, high], 0), nt) + (both + pltpu.roll(both, 64, 1))
    line = jnp.where(lane_of((128, 128)) < 64, line[:128], line[128:])
    pieces = [line[q * SLABS : (q + 1) * SLABS] for q in range(4)]
    for m in range(4):
        lines[pl.ds(m, SLABS, stride=4), :] = regroup(pieces, m)


def three(left_high, left_low, right):
    high, low = split(right)
    return dot(left_high, high) + (dot(left_high, low) + dot(left_low, high))


def filter_z(lines, factors, along_high, along_low, back):
    near = (lane_of((8, 128)) & 8) == 0
    own = []
    for pair in range(SETS // 2):
        rows = {}
        for m in range(4):
            first = lines[pl.ds(8 * pair + m, 8, stride=16), :]
            second = lines[pl.ds(8 * pair + 4 + m, 8, stride=16), :]
            rows[0, m] = jnp.where(near, first, pltpu.roll(second, 8, 1))
            rows[1, m] = jnp.where(near, pltpu.roll(first, 120, 1), second)
        own.append(jnp.concatenate([rows[zp, m] for zp in range(2) for m in range(4)], 0))
    own = jnp.concatenate(own, 1)
    group = lax.axis_index("zh")
    data = jnp.concatenate([jnp.where(group == zh, own, 0.0) for zh in range(GROUPS)], 0)
    freq = three(along_high[...], along_low[...], data)
    lane = lane_of((N, 128))
    sign = jnp.where(lane < 64, 1.0, -1.0)
    alone = (lax.axis_index(INSIDE) == 0) & ((lane & 56) == 0)
    kept = []
    for pair in range(SETS // 2):
        cosine = freq[:N, 128 * pair : 128 * pair + 128]
        sine = freq[N:, 128 * pair : 128 * pair + 128]
        mix = jnp.where(alone, 0.0, sign) if pair == 0 else sign
        scale = factors[:, 128 * pair : 128 * pair + 128]
        kept.append((scale * (cosine + mix * pltpu.roll(sine, 64, 1)), scale * (sine - mix * pltpu.roll(cosine, 64, 1))))
    kept_cosine, kept_sine = (jnp.concatenate([pieces[part] for pieces in kept], 1) for part in range(2))
    depth = three(along_high[:N, :], along_low[:N, :], kept_cosine) + three(along_high[N:, :], along_low[N:, :], kept_sine)
    for zh in range(GROUPS):
        for pair in range(SETS // 2):
            for m in range(4):
                row = 64 * zh + 8 * m
                even = depth[row : row + 8, 128 * pair : 128 * pair + 128]
                odd = depth[row + 32 : row + 40, 128 * pair : 128 * pair + 128]
                goal = 128 * zh + 8 * pair + m
                back[pl.ds(goal, 8, stride=16), :] = jnp.where(near, even, pltpu.roll(odd, 8, 1))
                back[pl.ds(goal + 4, 8, stride=16), :] = jnp.where(near, pltpu.roll(even, 120, 1), odd)


def inverse_x(lines, features, fwd_high, fwd_low, volume, sums, result, partial, sem):
    blocks = [sum(lines[pl.ds(128 * zh + m, SLABS, stride=4), :] for zh in range(GROUPS)) for m in range(4)]
    line = jnp.concatenate([regroup(blocks, q) for q in range(4)], 0).T
    line = jnp.concatenate([line[:64], line[64:]], 1)
    line = line * jnp.where((lane_of((ROWS, N)) & 127) == 0, 1.0 / (N * N), 2.0 / (N * N))
    high, low = split(line)
    both = dot(jnp.concatenate([high, low], 0), fwd_high[...])
    values = both[:ROWS] + (both[ROWS:] + dot(high, fwd_low[...]))
    result[...] = values
    leave = pltpu.make_async_copy(result, volume, sem)
    leave.start()

    def channels(step, carry):
        for k in range(8):
            c = step * 8 + k
            piece = features[pl.ds(pl.multiple_of(c * ROWS, ROWS), ROWS), :].astype(F32) * values
            piece = sum(piece[z * YP : (z + 1) * YP] for z in range(ZL))
            partial[pl.ds(pl.multiple_of(c * YP, YP), YP), :] = piece[:, :128] + piece[:, 128:]
        return carry

    lax.fori_loop(0, C // 8, channels, 0)
    total = sum(partial[pl.ds(y, C, stride=YP), :] for y in range(YP))
    total = jnp.concatenate([total, jnp.zeros((128 - C, 128), F32)], 0)
    high, low = split(total)
    rest = (total - high.astype(F32) - low.astype(F32)).astype(BF16)
    ones = jnp.ones((sums.shape[0], 128), BF16)
    nt = ((1,), (1,))
    sums[...] = dot(ones, high, nt) + (dot(ones, low, nt) + dot(ones, rest, nt))
    leave.wait()


def call(body, outs, spaces, scratch=(), cost=(0, 0)):
    whole = {"v": pl.BlockSpec(memory_space=pltpu.VMEM), "s": pl.BlockSpec(memory_space=pltpu.SMEM), "h": pl.BlockSpec(memory_space=pltpu.HBM)}
    ins, goals = spaces.split(">")
    return pl.pallas_call(
        body,
        out_shape=[jax.ShapeDtypeStruct(shape, kind) for shape, kind in outs],
        in_specs=[whole[space] for space in ins],
        out_specs=[whole[space] for space in goals],
        scratch_shapes=list(scratch),
        compiler_params=pltpu.CompilerParams(vmem_limit_bytes=VMEM_LIMIT),
        cost_estimate=pl.CostEstimate(flops=cost[0], bytes_accessed=cost[1], transcendentals=0),
    )


def hbm(array):
    return pltpu.with_memory_space_constraint(array, pltpu.HBM)


def on_device(sizes, features, target, out_weight, rotation, blocks, wedge):
    slab = tuple(name for name, _ in PARTS["slab"])
    features = features.reshape(C * ROWS, N)
    target = target.reshape(ROWS, N)
    fwd_high, fwd_low, along_high, along_low = [hbm(jnp.asarray(table)) for table in tables()]
    lines, features, fwd_high, fwd_low = call(
        forward_x,
        [((128, 128), F32), ((C * ROWS, N), BF16), (fwd_high.shape, BF16), (fwd_low.shape, BF16)],
        "hhhhh>vvvv",
        [pltpu.SMEM((C,), F32), pltpu.VMEM((ROWS, N), BF16), pltpu.SemaphoreType.DMA((4 + CHUNKS,))],
        (200_000_000, 3_000_000),
    )(hbm(out_weight), hbm(target), hbm(features), fwd_high, fwd_low)
    rotation, lines = lax.optimization_barrier((rotation, lines))
    factors, along_high, along_low = call(
        prepare,
        [((N, N), F32), (along_high.shape, BF16), (along_low.shape, BF16)],
        "shhhh>vvv",
        [pltpu.SMEM((2, NB), jnp.int32), pltpu.VMEM((N, N), jnp.int32), pltpu.SemaphoreType.DMA((4,))],
        (200_000_000, 3_000_000),
    )(rotation, hbm(blocks.T), hbm(wedge), along_high, along_low)
    lines = lax.all_to_all(lines.reshape(8, 16, 128), INSIDE, 0, 0, tiled=True).reshape(128, 128)
    (back,) = call(filter_z, [((GROUPS * 128, 128), F32)], "vvvv>v", (), (200_000_000, 2_000_000))(
        lines, factors, along_high, along_low
    )
    back = lax.all_to_all(back.reshape(SLABS, 16, 128), slab, 0, 0, tiled=True).reshape(GROUPS * 128, 128)
    far = math.prod(sizes[name] for name in FAR)
    near = math.prod(sizes[name] for name in NEAR)
    volume, sums = call(
        inverse_x,
        [((ROWS, N), F32), ((far, 128), F32)],
        "vvvv>hv",
        [pltpu.VMEM((ROWS, N), F32), pltpu.VMEM((C * YP, 128), F32), pltpu.SemaphoreType.DMA],
        (200_000_000, 3_000_000),
    )(back, features, fwd_high, fwd_low)
    sums = lax.all_to_all(sums.reshape(far, 1, 128), FAR, 0, 0, tiled=True)
    sums = jnp.sum(sums, 0, keepdims=True)
    sums = jnp.broadcast_to(sums, (near, 1, 128))
    sums = lax.all_to_all(sums, NEAR, 0, 0, tiled=True)
    w_grad = jnp.sum(sums, (0, 1))[:C] * (1.0 / (math.prod(sizes.values()) * ROWS * N))
    return volume.reshape(1, ZL, YP, N), w_grad


def solution(mesh):
    parts = PARTS["dp"] + PARTS["slab"]
    sizes = dict(parts)
    dp = tuple(name for name, _ in PARTS["dp"])
    slab = tuple(name for name, _ in PARTS["slab"])
    fine = Mesh(mesh.devices.reshape([size for _, size in parts]), tuple(sizes))
    in_specs = (P(dp, None, slab, None, None), P(dp, slab, None, None), P(), P(dp), P(), P())
    out_specs = (P(dp, slab, None, None), P())
    return jax.shard_map(
        functools.partial(on_device, sizes), mesh=fine, in_specs=in_specs, out_specs=out_specs, check_vma=False
    )
```

```python
import functools
import math

import jax
import jax.numpy as jnp
import numpy as np
from jax import lax
from jax.experimental import pallas as pl
from jax.experimental.pallas import tpu as pltpu
from jax.sharding import Mesh
from jax.sharding import PartitionSpec as P

N = 256
C = 64
BLK = 64
NB = 8
SLABS = 32
ZL = 8
YP = 8
ROWS = ZL * YP
CHUNKS = 8
PARTS = {"dp": (("y", 4), ("xh", 2), ("core", 2)), "slab": (("z", 16), ("xl", 2))}
NEAR = ("y", "xh")
FAR = ("core", "z", "xl")
HALF = SLABS // 2
FIRST_FAR = 17
FIRST_NEAR = 5

F32, BF16 = jnp.float32, jnp.bfloat16
VMEM_LIMIT = 16 * 1024 * 1024


def halves(table):
    high = table.astype(np.float32).astype(BF16)
    low = (table - high.astype(np.float64)).astype(np.float32).astype(BF16)
    return high, low


def tables():
    step = 2.0 * math.pi / N
    space = np.arange(N)
    quad, slab = np.meshgrid(np.arange(4), np.arange(SLABS), indexing="ij")
    freq = (4 * ((slab + HALF) % SLABS) + quad).reshape(-1)
    phase = (freq[:, None] * space[None, :]) % N * step
    real, imag = np.cos(phase), -np.sin(phase)
    imag[freq == 0] = np.cos(math.pi * space)
    zp, m, i = np.meshgrid(np.arange(2), np.arange(4), np.arange(SLABS), indexing="ij")
    depth = (8 * ((i + HALF) % SLABS) + 2 * m + zp).reshape(-1)
    phase = (depth[:, None] * depth[None, :]) % N * step
    along = np.concatenate([np.cos(phase), np.sin(phase)], 0)
    return halves(np.concatenate([real, imag], 0)) + halves(along)


def split(values):
    high = values.astype(BF16)
    return high, (values - high.astype(F32)).astype(BF16)


def dot(left, right, dims=((1,), (0,))):
    return lax.dot_general(left, right, (dims, ((), ())), preferred_element_type=F32)


def lane_of(shape):
    return lax.broadcasted_iota(jnp.int32, shape, 1)


def regroup(pieces, to):
    group = (lane_of(pieces[0].shape) >> 4) & 3
    result = None
    for source in range(4):
        moved = pieces[source] if source == to else pltpu.roll(pieces[source], (16 * (source - to)) % 128, 1)
        result = moved if result is None else jnp.where(group == source, moved, result)
    return result


def slab_index():
    return lax.axis_index(tuple(name for name, _ in PARTS["slab"])).astype(jnp.int32)


def filter_weights(turn, place, blocks, wedge, out):
    kz = lax.broadcasted_iota(jnp.int32, (8, N), 0)
    kx = lane_of((8, N)) >> 6
    listed = jnp.zeros((8, N), jnp.bool_)
    for n in range(NB):
        listed = listed | ((kz == blocks[0, n]) & (kx == blocks[1, n]))
    listed = listed.astype(F32)
    mask = jnp.concatenate(
        [wedge[a * BLK : (a + 1) * BLK, :].astype(F32) * listed[a : a + 1, :] for a in range(N // BLK)], 0
    ).astype(BF16)
    lane = lane_of((N, 128))
    row = lax.broadcasted_iota(jnp.int32, (N, 128), 0)
    quad = (lane >> 4) & 3
    freq = 4 * place + quad
    freq = jnp.where((freq == 0) & (lane >= 64), N // 2, freq)
    plus = (row == freq).astype(F32).astype(BF16)
    minus = (row == ((N - freq) & (N - 1))).astype(F32).astype(BF16)
    picks = jnp.concatenate([plus, minus], 1)
    odd = (turn & 1) == 1
    plain = dot(mask, picks)
    other = dot(mask, picks, ((0,), (0,)))
    direct = jnp.where(odd, other[:, 128:], plain[:, :128])
    mirror = jnp.where(odd, other[:, :128], plain[:, 128:]).astype(BF16)
    r = lax.broadcasted_iota(jnp.int32, (N, N), 0)
    p = (8 * ((r & 31) + HALF) + 2 * ((r >> 5) & 3) + (r >> 7)) & (N - 1)
    k = lane_of((N, N))
    keep = (k == p).astype(F32).astype(BF16)
    flip = (((p + k) & (N - 1)) == 0).astype(F32).astype(BF16)
    out[...] = dot(keep, direct.astype(BF16)) + dot(flip, mirror)


def prepare(turn, blocks_hbm, wedge_hbm, high_hbm, low_hbm, factors, high, low, blocks, wedge, sems):
    pairs = [(blocks_hbm, blocks), (wedge_hbm, wedge), (high_hbm, high), (low_hbm, low)]
    copies = [pltpu.make_async_copy(source, goal, sems.at[n]) for n, (source, goal) in enumerate(pairs)]
    for copy in copies:
        copy.start()
    for copy in copies[:2]:
        copy.wait()
    filter_weights(turn[0], slab_index(), blocks, wedge, factors)
    for copy in copies[2:]:
        copy.wait()


def forward_x(weight_hbm, target_hbm, features_hbm, high_hbm, low_hbm, lines, features, fwd_high, fwd_low, weight, target, sems):
    part = C * ROWS // CHUNKS
    pairs = [(weight_hbm, weight), (target_hbm, target)]
    for k in range(CHUNKS):
        rows = pl.ds(k * part, part)
        pairs.append((features_hbm.at[rows], features.at[rows]))
    pairs += [(high_hbm, fwd_high), (low_hbm, fwd_low)]
    copies = [pltpu.make_async_copy(source, goal, sems.at[n]) for n, (source, goal) in enumerate(pairs)]
    for copy in copies:
        copy.start()
    for copy in copies[:2]:
        copy.wait()
    total = -target[...].astype(F32)
    for k in range(CHUNKS):
        copies[2 + k].wait()
        for c in range(k * C // CHUNKS, (k + 1) * C // CHUNKS):
            total = total + weight[c] * features[c * ROWS : (c + 1) * ROWS, :].astype(F32)
    high, low = split(total)
    nt = ((1,), (1,))
    for copy in copies[2 + CHUNKS :]:
        copy.wait()
    both = dot(fwd_high[...], jnp.concatenate([high, low], 0), nt)
    line = dot(fwd_low[...], jnp.concatenate([high, high], 0), nt) + (both + pltpu.roll(both, 64, 1))
    line = jnp.where(lane_of((128, 128)) < 64, line[:128], line[128:])
    pieces = [line[q * SLABS : (q + 1) * SLABS] for q in range(4)]
    for m in range(4):
        lines[pl.ds(m, SLABS, stride=4), :] = regroup(pieces, m)


def three(left_high, left_low, right):
    high, low = split(right)
    both = dot(left_high, jnp.concatenate([high, low], 1))
    return dot(left_low, high) + (both[:, :128] + both[:, 128:])


def filter_z(lines, factors, along_high, along_low, back):
    even = jnp.concatenate([lines[pl.ds(m, SLABS, stride=4), :] for m in range(4)], 0)
    data = jnp.concatenate([even, pltpu.roll(even, 120, 1)], 0)
    freq = three(along_high[...], along_low[...], data)
    cosine, sine = freq[:N], freq[N:]
    lane = lane_of((N, 128))
    sign = jnp.where(lane < 64, 1.0, -1.0)
    sign = jnp.where((slab_index() == 0) & (((lane >> 4) & 3) == 0), 0.0, sign)
    scale = factors[...]
    kept_cosine = scale * (cosine + sign * pltpu.roll(sine, 64, 1))
    kept_sine = scale * (sine - sign * pltpu.roll(cosine, 64, 1))
    depth = three(along_high[:N, :], along_low[:N, :], kept_cosine) + three(along_high[N:, :], along_low[N:, :], kept_sine)
    lane = lane_of((SLABS, 128))
    for m in range(4):
        first = depth[m * SLABS : (m + 1) * SLABS]
        second = depth[128 + m * SLABS : 128 + (m + 1) * SLABS]
        back[pl.ds(m, SLABS, stride=4), :] = jnp.where((lane & 8) == 0, first, pltpu.roll(second, 8, 1))


def inverse_x(lines, features, fwd_high, fwd_low, volume, sums, result, partial, sem):
    blocks = [lines[pl.ds(m, SLABS, stride=4), :] for m in range(4)]
    line = jnp.concatenate([regroup(blocks, q) for q in range(4)], 0).T
    line = jnp.concatenate([line[:64], line[64:]], 1)
    line = line * jnp.where((lane_of((ROWS, N)) & 127) == HALF, 1.0 / (N * N), 2.0 / (N * N))
    high, low = split(line)
    both = dot(jnp.concatenate([high, low], 0), fwd_high[...])
    values = both[:ROWS] + (both[ROWS:] + dot(high, fwd_low[...]))
    result[...] = values
    leave = pltpu.make_async_copy(result, volume, sem)
    leave.start()

    def channels(step, carry):
        for k in range(8):
            c = step * 8 + k
            piece = features[pl.ds(pl.multiple_of(c * ROWS, ROWS), ROWS), :].astype(F32) * values
            piece = sum(piece[z * YP : (z + 1) * YP] for z in range(ZL))
            partial[pl.ds(pl.multiple_of(c * YP, YP), YP), :] = piece[:, :128] + piece[:, 128:]
        return carry

    lax.fori_loop(0, C // 8, channels, 0)
    total = sum(partial[pl.ds(y, C, stride=YP), :] for y in range(YP))
    total = jnp.concatenate([total, jnp.zeros((128 - C, 128), F32)], 0)
    high, low = split(total)
    rest = (total - high.astype(F32) - low.astype(F32)).astype(BF16)
    ones = jnp.ones((sums.shape[0], 128), BF16)
    nt = ((1,), (1,))
    sums[...] = dot(ones, high, nt) + (dot(ones, low, nt) + dot(ones, rest, nt))
    leave.wait()


def call(body, outs, spaces, scratch=(), cost=(0, 0)):
    whole = {"v": pl.BlockSpec(memory_space=pltpu.VMEM), "s": pl.BlockSpec(memory_space=pltpu.SMEM), "h": pl.BlockSpec(memory_space=pltpu.HBM)}
    ins, goals = spaces.split(">")
    return pl.pallas_call(
        body,
        out_shape=[jax.ShapeDtypeStruct(shape, kind) for shape, kind in outs],
        in_specs=[whole[space] for space in ins],
        out_specs=[whole[space] for space in goals],
        scratch_shapes=list(scratch),
        compiler_params=pltpu.CompilerParams(vmem_limit_bytes=VMEM_LIMIT),
        cost_estimate=pl.CostEstimate(flops=cost[0], bytes_accessed=cost[1], transcendentals=0),
    )


def exchange(array, names, size, first):
    order = [[(first + n) % size for n in range(size)]]
    return lax.all_to_all(array, names, 0, 0, axis_index_groups=order, tiled=True)


def hbm(array):
    return pltpu.with_memory_space_constraint(array, pltpu.HBM)


def on_device(sizes, features, target, out_weight, rotation, blocks, wedge):
    slab = tuple(name for name, _ in PARTS["slab"])
    features = features.reshape(C * ROWS, N)
    target = target.reshape(ROWS, N)
    fwd_high, fwd_low, along_high, along_low = [hbm(jnp.asarray(table)) for table in tables()]
    lines, features, fwd_high, fwd_low = call(
        forward_x,
        [((128, 128), F32), ((C * ROWS, N), BF16), (fwd_high.shape, BF16), (fwd_low.shape, BF16)],
        "hhhhh>vvvv",
        [pltpu.SMEM((C,), F32), pltpu.VMEM((ROWS, N), BF16), pltpu.SemaphoreType.DMA((4 + CHUNKS,))],
        (200_000_000, 3_000_000),
    )(hbm(out_weight), hbm(target), hbm(features), fwd_high, fwd_low)
    rotation, lines = lax.optimization_barrier((rotation, lines))
    factors, along_high, along_low = call(
        prepare,
        [((N, 128), F32), (along_high.shape, BF16), (along_low.shape, BF16)],
        "shhhh>vvv",
        [pltpu.SMEM((2, NB), jnp.int32), pltpu.VMEM((N, N), jnp.int32), pltpu.SemaphoreType.DMA((4,))],
        (200_000_000, 3_000_000),
    )(rotation, hbm(blocks.T), hbm(wedge), along_high, along_low)
    lines = exchange(lines.reshape(SLABS, 4, 128), slab, SLABS, HALF).reshape(128, 128)
    (back,) = call(filter_z, [((128, 128), F32)], "vvvv>v", (), (200_000_000, 2_000_000))(
        lines, factors, along_high, along_low
    )
    back = exchange(back.reshape(SLABS, 4, 128), slab, SLABS, HALF).reshape(128, 128)
    far = math.prod(sizes[name] for name in FAR)
    near = math.prod(sizes[name] for name in NEAR)
    volume, sums = call(
        inverse_x,
        [((ROWS, N), F32), ((far, 128), F32)],
        "vvvv>hv",
        [pltpu.VMEM((ROWS, N), F32), pltpu.VMEM((C * YP, 128), F32), pltpu.SemaphoreType.DMA],
        (200_000_000, 3_000_000),
    )(back, features, fwd_high, fwd_low)
    sums = exchange(sums.reshape(far, 1, 128), FAR, far, FIRST_FAR % far)
    sums = jnp.sum(sums, 0, keepdims=True)
    sums = jnp.broadcast_to(sums, (near, 1, 128))
    sums = exchange(sums, NEAR, near, FIRST_NEAR % near)
    w_grad = jnp.sum(sums, (0, 1))[:C] * (1.0 / (math.prod(sizes.values()) * ROWS * N))
    return volume.reshape(1, ZL, YP, N), w_grad


def solution(mesh):
    parts = PARTS["dp"] + PARTS["slab"]
    sizes = dict(parts)
    dp = tuple(name for name, _ in PARTS["dp"])
    slab = tuple(name for name, _ in PARTS["slab"])
    fine = Mesh(mesh.devices.reshape([size for _, size in parts]), tuple(sizes))
    in_specs = (P(dp, None, slab, None, None), P(dp, slab, None, None), P(), P(dp), P(), P())
    out_specs = (P(dp, slab, None, None), P())
    return jax.shard_map(
        functools.partial(on_device, sizes), mesh=fine, in_specs=in_specs, out_specs=out_specs, check_vma=False
    )
```

```python
import functools
import math

import jax
import jax.numpy as jnp
import numpy as np
from jax import lax
from jax.experimental import pallas as pl
from jax.experimental.pallas import tpu as pltpu
from jax.sharding import Mesh
from jax.sharding import PartitionSpec as P

N = 256
C = 64
BLK = 64
NB = 8
SLABS = 32
ZL = 8
YP = 8
ROWS = ZL * YP
CHUNKS = 8
PARTS = {"dp": (("y", 4), ("xh", 2), ("core", 2)), "slab": (("z", 16), ("xl", 2))}
NEAR = ("y", "xh", "xl")
FAR = ("core", "z")
HALF = SLABS // 2
FIRST_FAR = 8
FIRST_NEAR = 10

F32, BF16 = jnp.float32, jnp.bfloat16
VMEM_LIMIT = 16 * 1024 * 1024


def halves(table):
    high = table.astype(np.float32).astype(BF16)
    low = (table - high.astype(np.float64)).astype(np.float32).astype(BF16)
    return high, low


def tables():
    step = 2.0 * math.pi / N
    space = np.arange(N)
    quad, slab = np.meshgrid(np.arange(4), np.arange(SLABS), indexing="ij")
    freq = (4 * ((slab + HALF) % SLABS) + quad).reshape(-1)
    phase = (freq[:, None] * space[None, :]) % N * step
    real, imag = np.cos(phase), -np.sin(phase)
    imag[freq == 0] = np.cos(math.pi * space)
    zp, m, i = np.meshgrid(np.arange(2), np.arange(4), np.arange(SLABS), indexing="ij")
    depth = (8 * ((i + HALF) % SLABS) + 2 * m + zp).reshape(-1)
    phase = (depth[:, None] * depth[None, :]) % N * step
    along = np.concatenate([np.cos(phase), np.sin(phase)], 0)
    return halves(np.concatenate([real, imag], 0)) + halves(along)


def split(values):
    high = values.astype(BF16)
    return high, (values - high.astype(F32)).astype(BF16)


def dot(left, right, dims=((1,), (0,))):
    return lax.dot_general(left, right, (dims, ((), ())), preferred_element_type=F32)


def lane_of(shape):
    return lax.broadcasted_iota(jnp.int32, shape, 1)


def regroup(pieces, to):
    group = (lane_of(pieces[0].shape) >> 4) & 3
    result = None
    for source in range(4):
        moved = pieces[source] if source == to else pltpu.roll(pieces[source], (16 * (source - to)) % 128, 1)
        result = moved if result is None else jnp.where(group == source, moved, result)
    return result


def slab_index():
    return lax.axis_index(tuple(name for name, _ in PARTS["slab"])).astype(jnp.int32)


def filter_weights(turn, place, blocks, wedge, out):
    kz = lax.broadcasted_iota(jnp.int32, (8, N), 0)
    kx = lane_of((8, N)) >> 6
    listed = jnp.zeros((8, N), jnp.bool_)
    for n in range(NB):
        listed = listed | ((kz == blocks[0, n]) & (kx == blocks[1, n]))
    listed = listed.astype(F32)
    mask = jnp.concatenate(
        [wedge[a * BLK : (a + 1) * BLK, :].astype(F32) * listed[a : a + 1, :] for a in range(N // BLK)], 0
    ).astype(BF16)
    lane = lane_of((N, 128))
    row = lax.broadcasted_iota(jnp.int32, (N, 128), 0)
    quad = (lane >> 4) & 3
    freq = 4 * place + quad
    freq = jnp.where((freq == 0) & (lane >= 64), N // 2, freq)
    plus = (row == freq).astype(F32).astype(BF16)
    minus = (row == ((N - freq) & (N - 1))).astype(F32).astype(BF16)
    picks = jnp.concatenate([plus, minus], 1)
    odd = (turn & 1) == 1
    plain = dot(mask, picks)
    other = dot(mask, picks, ((0,), (0,)))
    direct = jnp.where(odd, other[:, 128:], plain[:, :128])
    mirror = jnp.where(odd, other[:, :128], plain[:, 128:]).astype(BF16)
    r = lax.broadcasted_iota(jnp.int32, (N, N), 0)
    p = (8 * ((r & 31) + HALF) + 2 * ((r >> 5) & 3) + (r >> 7)) & (N - 1)
    k = lane_of((N, N))
    keep = (k == p).astype(F32).astype(BF16)
    flip = (((p + k) & (N - 1)) == 0).astype(F32).astype(BF16)
    out[...] = dot(keep, direct.astype(BF16)) + dot(flip, mirror)


def prepare(turn, blocks_hbm, wedge_hbm, high_hbm, low_hbm, factors, high, low, blocks, wedge, sems):
    pairs = [(blocks_hbm, blocks), (wedge_hbm, wedge), (high_hbm, high), (low_hbm, low)]
    copies = [pltpu.make_async_copy(source, goal, sems.at[n]) for n, (source, goal) in enumerate(pairs)]
    for copy in copies:
        copy.start()
    for copy in copies[:2]:
        copy.wait()
    filter_weights(turn[0], slab_index(), blocks, wedge, factors)
    for copy in copies[2:]:
        copy.wait()


def forward_x(weight_hbm, target_hbm, features_hbm, high_hbm, low_hbm, lines, features, fwd_high, fwd_low, weight, target, sems):
    part = C * ROWS // CHUNKS
    pairs = [(weight_hbm, weight), (target_hbm, target)]
    for k in range(CHUNKS):
        rows = pl.ds(k * part, part)
        pairs.append((features_hbm.at[rows], features.at[rows]))
    pairs += [(high_hbm, fwd_high), (low_hbm, fwd_low)]
    copies = [pltpu.make_async_copy(source, goal, sems.at[n]) for n, (source, goal) in enumerate(pairs)]
    for copy in copies:
        copy.start()
    for copy in copies[:2]:
        copy.wait()
    total = -target[...].astype(F32)
    for k in range(CHUNKS):
        copies[2 + k].wait()
        for c in range(k * C // CHUNKS, (k + 1) * C // CHUNKS):
            total = total + weight[c] * features[c * ROWS : (c + 1) * ROWS, :].astype(F32)
    high, low = split(total)
    nt = ((1,), (1,))
    for copy in copies[2 + CHUNKS :]:
        copy.wait()
    both = dot(fwd_high[...], jnp.concatenate([high, low], 0), nt)
    line = dot(fwd_low[...], jnp.concatenate([high, high], 0), nt) + (both + pltpu.roll(both, 64, 1))
    line = jnp.where(lane_of((128, 128)) < 64, line[:128], line[128:])
    pieces = [line[q * SLABS : (q + 1) * SLABS] for q in range(4)]
    for m in range(4):
        lines[pl.ds(m, SLABS, stride=4), :] = regroup(pieces, m)


def three(left_high, left_low, right):
    high, low = split(right)
    both = dot(left_high, jnp.concatenate([high, low], 1))
    return dot(left_low, high) + (both[:, :128] + both[:, 128:])


def filter_z(lines, factors, along_high, along_low, back):
    even = jnp.concatenate([lines[pl.ds(m, SLABS, stride=4), :] for m in range(4)], 0)
    data = jnp.concatenate([even, pltpu.roll(even, 120, 1)], 0)
    freq = three(along_high[...], along_low[...], data)
    cosine, sine = freq[:N], freq[N:]
    lane = lane_of((N, 128))
    sign = jnp.where(lane < 64, 1.0, -1.0)
    sign = jnp.where((slab_index() == 0) & (((lane >> 4) & 3) == 0), 0.0, sign)
    scale = factors[...]
    kept_cosine = scale * (cosine + sign * pltpu.roll(sine, 64, 1))
    kept_sine = scale * (sine - sign * pltpu.roll(cosine, 64, 1))
    depth = three(along_high[:N, :], along_low[:N, :], kept_cosine) + three(along_high[N:, :], along_low[N:, :], kept_sine)
    lane = lane_of((SLABS, 128))
    for m in range(4):
        first = depth[m * SLABS : (m + 1) * SLABS]
        second = depth[128 + m * SLABS : 128 + (m + 1) * SLABS]
        back[pl.ds(m, SLABS, stride=4), :] = jnp.where((lane & 8) == 0, first, pltpu.roll(second, 8, 1))


def inverse_x(lines, features, fwd_high, fwd_low, volume, sums, result, partial, sem):
    blocks = [lines[pl.ds(m, SLABS, stride=4), :] for m in range(4)]
    line = jnp.concatenate([regroup(blocks, q) for q in range(4)], 0).T
    line = jnp.concatenate([line[:64], line[64:]], 1)
    line = line * jnp.where((lane_of((ROWS, N)) & 127) == HALF, 1.0 / (N * N), 2.0 / (N * N))
    high, low = split(line)
    both = dot(jnp.concatenate([high, low], 0), fwd_high[...])
    values = both[:ROWS] + (both[ROWS:] + dot(high, fwd_low[...]))
    result[...] = values
    leave = pltpu.make_async_copy(result, volume, sem)
    leave.start()

    def channels(step, carry):
        for k in range(8):
            c = step * 8 + k
            piece = features[pl.ds(pl.multiple_of(c * ROWS, ROWS), ROWS), :].astype(F32) * values
            piece = sum(piece[z * YP : (z + 1) * YP] for z in range(ZL))
            partial[pl.ds(pl.multiple_of(c * YP, YP), YP), :] = piece[:, :128] + piece[:, 128:]
        return carry

    lax.fori_loop(0, C // 8, channels, 0)
    total = sum(partial[pl.ds(y, C, stride=YP), :] for y in range(YP))
    total = jnp.concatenate([total, jnp.zeros((128 - C, 128), F32)], 0)
    high, low = split(total)
    rest = (total - high.astype(F32) - low.astype(F32)).astype(BF16)
    ones = jnp.ones((sums.shape[0], 128), BF16)
    nt = ((1,), (1,))
    sums[...] = dot(ones, high, nt) + (dot(ones, low, nt) + dot(ones, rest, nt))
    leave.wait()


def call(body, outs, spaces, scratch=(), cost=(0, 0)):
    whole = {"v": pl.BlockSpec(memory_space=pltpu.VMEM), "s": pl.BlockSpec(memory_space=pltpu.SMEM), "h": pl.BlockSpec(memory_space=pltpu.HBM)}
    ins, goals = spaces.split(">")
    return pl.pallas_call(
        body,
        out_shape=[jax.ShapeDtypeStruct(shape, kind) for shape, kind in outs],
        in_specs=[whole[space] for space in ins],
        out_specs=[whole[space] for space in goals],
        scratch_shapes=list(scratch),
        compiler_params=pltpu.CompilerParams(vmem_limit_bytes=VMEM_LIMIT),
        cost_estimate=pl.CostEstimate(flops=cost[0], bytes_accessed=cost[1], transcendentals=0),
    )


def exchange(array, names, size, first):
    order = [[(first + n) % size for n in range(size)]]
    return lax.all_to_all(array, names, 0, 0, axis_index_groups=order, tiled=True)


def hbm(array):
    return pltpu.with_memory_space_constraint(array, pltpu.HBM)


def on_device(sizes, features, target, out_weight, rotation, blocks, wedge):
    slab = tuple(name for name, _ in PARTS["slab"])
    features = features.reshape(C * ROWS, N)
    target = target.reshape(ROWS, N)
    fwd_high, fwd_low, along_high, along_low = [hbm(jnp.asarray(table)) for table in tables()]
    lines, features, fwd_high, fwd_low = call(
        forward_x,
        [((128, 128), F32), ((C * ROWS, N), BF16), (fwd_high.shape, BF16), (fwd_low.shape, BF16)],
        "hhhhh>vvvv",
        [pltpu.SMEM((C,), F32), pltpu.VMEM((ROWS, N), BF16), pltpu.SemaphoreType.DMA((4 + CHUNKS,))],
        (200_000_000, 3_000_000),
    )(hbm(out_weight), hbm(target), hbm(features), fwd_high, fwd_low)
    rotation, lines = lax.optimization_barrier((rotation, lines))
    factors, along_high, along_low = call(
        prepare,
        [((N, 128), F32), (along_high.shape, BF16), (along_low.shape, BF16)],
        "shhhh>vvv",
        [pltpu.SMEM((2, NB), jnp.int32), pltpu.VMEM((N, N), jnp.int32), pltpu.SemaphoreType.DMA((4,))],
        (200_000_000, 3_000_000),
    )(rotation, hbm(blocks.T), hbm(wedge), along_high, along_low)
    lines = exchange(lines.reshape(SLABS, 4, 128), slab, SLABS, HALF).reshape(128, 128)
    (back,) = call(filter_z, [((128, 128), F32)], "vvvv>v", (), (200_000_000, 2_000_000))(
        lines, factors, along_high, along_low
    )
    back = exchange(back.reshape(SLABS, 4, 128), slab, SLABS, HALF).reshape(128, 128)
    far = math.prod(sizes[name] for name in FAR)
    near = math.prod(sizes[name] for name in NEAR)
    volume, sums = call(
        inverse_x,
        [((ROWS, N), F32), ((far, 128), F32)],
        "vvvv>hv",
        [pltpu.VMEM((ROWS, N), F32), pltpu.VMEM((C * YP, 128), F32), pltpu.SemaphoreType.DMA],
        (200_000_000, 3_000_000),
    )(back, features, fwd_high, fwd_low)
    sums = exchange(sums.reshape(far, 1, 128), FAR, far, FIRST_FAR % far)
    sums = jnp.sum(sums, 0, keepdims=True)
    sums = jnp.broadcast_to(sums, (near, 1, 128))
    sums = exchange(sums, NEAR, near, FIRST_NEAR % near)
    w_grad = jnp.sum(sums, (0, 1))[:C] * (1.0 / (math.prod(sizes.values()) * ROWS * N))
    return volume.reshape(1, ZL, YP, N), w_grad


def solution(mesh):
    parts = PARTS["dp"] + PARTS["slab"]
    sizes = dict(parts)
    dp = tuple(name for name, _ in PARTS["dp"])
    slab = tuple(name for name, _ in PARTS["slab"])
    fine = Mesh(mesh.devices.reshape([size for _, size in parts]), tuple(sizes))
    in_specs = (P(dp, None, slab, None, None), P(dp, slab, None, None), P(), P(dp), P(), P())
    out_specs = (P(dp, slab, None, None), P())
    return jax.shard_map(
        functools.partial(on_device, sizes), mesh=fine, in_specs=in_specs, out_specs=out_specs, check_vma=False
    )
```

```python
import functools
import math

import jax
import jax.numpy as jnp
import numpy as np
from jax import lax
from jax.experimental import pallas as pl
from jax.experimental.pallas import tpu as pltpu
from jax.sharding import Mesh
from jax.sharding import PartitionSpec as P

N = 256
C = 64
BLK = 64
NB = 8
SLABS = 32
ZL = 8
YP = 8
ROWS = ZL * YP
CHUNKS = 8
PARTS = {"dp": (("y", 4), ("xh", 2), ("core", 2)), "slab": (("z", 16), ("xl", 2))}
NEAR = ("y", "xh", "xl", "core")
FAR = ("z",)
HALF = SLABS // 2
FIRST_FAR = 8
FIRST_NEAR = 20

F32, BF16 = jnp.float32, jnp.bfloat16
VMEM_LIMIT = 16 * 1024 * 1024


def halves(table):
    high = table.astype(np.float32).astype(BF16)
    low = (table - high.astype(np.float64)).astype(np.float32).astype(BF16)
    return high, low


def tables():
    step = 2.0 * math.pi / N
    space = np.arange(N)
    quad, slab = np.meshgrid(np.arange(4), np.arange(SLABS), indexing="ij")
    freq = (4 * ((slab + HALF) % SLABS) + quad).reshape(-1)
    phase = (freq[:, None] * space[None, :]) % N * step
    real, imag = np.cos(phase), -np.sin(phase)
    imag[freq == 0] = np.cos(math.pi * space)
    zp, m, i = np.meshgrid(np.arange(2), np.arange(4), np.arange(SLABS), indexing="ij")
    depth = (8 * ((i + HALF) % SLABS) + 2 * m + zp).reshape(-1)
    phase = (depth[:, None] * depth[None, :]) % N * step
    along = np.concatenate([np.cos(phase), np.sin(phase)], 0)
    return halves(np.concatenate([real, imag], 0)) + halves(along)


def split(values):
    high = values.astype(BF16)
    return high, (values - high.astype(F32)).astype(BF16)


def dot(left, right, dims=((1,), (0,))):
    return lax.dot_general(left, right, (dims, ((), ())), preferred_element_type=F32)


def lane_of(shape):
    return lax.broadcasted_iota(jnp.int32, shape, 1)


def regroup(pieces, to):
    group = (lane_of(pieces[0].shape) >> 4) & 3
    result = None
    for source in range(4):
        moved = pieces[source] if source == to else pltpu.roll(pieces[source], (16 * (source - to)) % 128, 1)
        result = moved if result is None else jnp.where(group == source, moved, result)
    return result


def slab_index():
    return lax.axis_index(tuple(name for name, _ in PARTS["slab"])).astype(jnp.int32)


def filter_weights(turn, place, blocks, wedge, out):
    kz = lax.broadcasted_iota(jnp.int32, (8, N), 0)
    kx = lane_of((8, N)) >> 6
    listed = jnp.zeros((8, N), jnp.bool_)
    for n in range(NB):
        listed = listed | ((kz == blocks[0, n]) & (kx == blocks[1, n]))
    listed = listed.astype(F32)
    mask = jnp.concatenate(
        [wedge[a * BLK : (a + 1) * BLK, :].astype(F32) * listed[a : a + 1, :] for a in range(N // BLK)], 0
    ).astype(BF16)
    lane = lane_of((N, 128))
    row = lax.broadcasted_iota(jnp.int32, (N, 128), 0)
    quad = (lane >> 4) & 3
    freq = 4 * place + quad
    freq = jnp.where((freq == 0) & (lane >= 64), N // 2, freq)
    plus = (row == freq).astype(F32).astype(BF16)
    minus = (row == ((N - freq) & (N - 1))).astype(F32).astype(BF16)
    picks = jnp.concatenate([plus, minus], 1)
    odd = (turn & 1) == 1
    plain = dot(mask, picks)
    other = dot(mask, picks, ((0,), (0,)))
    direct = jnp.where(odd, other[:, 128:], plain[:, :128])
    mirror = jnp.where(odd, other[:, :128], plain[:, 128:]).astype(BF16)
    r = lax.broadcasted_iota(jnp.int32, (N, N), 0)
    p = (8 * ((r & 31) + HALF) + 2 * ((r >> 5) & 3) + (r >> 7)) & (N - 1)
    k = lane_of((N, N))
    keep = (k == p).astype(F32).astype(BF16)
    flip = (((p + k) & (N - 1)) == 0).astype(F32).astype(BF16)
    out[...] = dot(keep, direct.astype(BF16)) + dot(flip, mirror)


def prepare(turn, blocks_hbm, wedge_hbm, high_hbm, low_hbm, factors, high, low, blocks, wedge, sems):
    pairs = [(blocks_hbm, blocks), (wedge_hbm, wedge), (high_hbm, high), (low_hbm, low)]
    copies = [pltpu.make_async_copy(source, goal, sems.at[n]) for n, (source, goal) in enumerate(pairs)]
    for copy in copies:
        copy.start()
    for copy in copies[:2]:
        copy.wait()
    filter_weights(turn[0], slab_index(), blocks, wedge, factors)
    for copy in copies[2:]:
        copy.wait()


def forward_x(weight_hbm, target_hbm, features_hbm, high_hbm, low_hbm, lines, features, fwd_high, fwd_low, weight, target, sems):
    part = C * ROWS // CHUNKS
    pairs = [(weight_hbm, weight), (target_hbm, target)]
    for k in range(CHUNKS):
        rows = pl.ds(k * part, part)
        pairs.append((features_hbm.at[rows], features.at[rows]))
    pairs += [(high_hbm, fwd_high), (low_hbm, fwd_low)]
    copies = [pltpu.make_async_copy(source, goal, sems.at[n]) for n, (source, goal) in enumerate(pairs)]
    for copy in copies:
        copy.start()
    for copy in copies[:2]:
        copy.wait()
    total = -target[...].astype(F32)
    for k in range(CHUNKS):
        copies[2 + k].wait()
        for c in range(k * C // CHUNKS, (k + 1) * C // CHUNKS):
            total = total + weight[c] * features[c * ROWS : (c + 1) * ROWS, :].astype(F32)
    high, low = split(total)
    nt = ((1,), (1,))
    for copy in copies[2 + CHUNKS :]:
        copy.wait()
    both = dot(fwd_high[...], jnp.concatenate([high, low], 0), nt)
    line = dot(fwd_low[...], jnp.concatenate([high, high], 0), nt) + (both + pltpu.roll(both, 64, 1))
    line = jnp.where(lane_of((128, 128)) < 64, line[:128], line[128:])
    pieces = [line[q * SLABS : (q + 1) * SLABS] for q in range(4)]
    for m in range(4):
        lines[pl.ds(m, SLABS, stride=4), :] = regroup(pieces, m)


def three(left_high, left_low, right):
    high, low = split(right)
    both = dot(left_high, jnp.concatenate([high, low], 1))
    return dot(left_low, high) + (both[:, :128] + both[:, 128:])


def filter_z(lines, factors, along_high, along_low, back):
    even = jnp.concatenate([lines[pl.ds(m, SLABS, stride=4), :] for m in range(4)], 0)
    data = jnp.concatenate([even, pltpu.roll(even, 120, 1)], 0)
    freq = three(along_high[...], along_low[...], data)
    cosine, sine = freq[:N], freq[N:]
    lane = lane_of((N, 128))
    sign = jnp.where(lane < 64, 1.0, -1.0)
    sign = jnp.where((slab_index() == 0) & (((lane >> 4) & 3) == 0), 0.0, sign)
    scale = factors[...]
    kept_cosine = scale * (cosine + sign * pltpu.roll(sine, 64, 1))
    kept_sine = scale * (sine - sign * pltpu.roll(cosine, 64, 1))
    depth = three(along_high[:N, :], along_low[:N, :], kept_cosine) + three(along_high[N:, :], along_low[N:, :], kept_sine)
    lane = lane_of((SLABS, 128))
    for m in range(4):
        first = depth[m * SLABS : (m + 1) * SLABS]
        second = depth[128 + m * SLABS : 128 + (m + 1) * SLABS]
        back[pl.ds(m, SLABS, stride=4), :] = jnp.where((lane & 8) == 0, first, pltpu.roll(second, 8, 1))


def inverse_x(lines, features, fwd_high, fwd_low, volume, sums, result, partial, sem):
    blocks = [lines[pl.ds(m, SLABS, stride=4), :] for m in range(4)]
    line = jnp.concatenate([regroup(blocks, q) for q in range(4)], 0).T
    line = jnp.concatenate([line[:64], line[64:]], 1)
    line = line * jnp.where((lane_of((ROWS, N)) & 127) == HALF, 1.0 / (N * N), 2.0 / (N * N))
    high, low = split(line)
    both = dot(jnp.concatenate([high, low], 0), fwd_high[...])
    values = both[:ROWS] + (both[ROWS:] + dot(high, fwd_low[...]))
    result[...] = values
    leave = pltpu.make_async_copy(result, volume, sem)
    leave.start()

    def channels(step, carry):
        for k in range(8):
            c = step * 8 + k
            piece = features[pl.ds(pl.multiple_of(c * ROWS, ROWS), ROWS), :].astype(F32) * values
            piece = sum(piece[z * YP : (z + 1) * YP] for z in range(ZL))
            partial[pl.ds(pl.multiple_of(c * YP, YP), YP), :] = piece[:, :128] + piece[:, 128:]
        return carry

    lax.fori_loop(0, C // 8, channels, 0)
    total = sum(partial[pl.ds(y, C, stride=YP), :] for y in range(YP))
    total = jnp.concatenate([total, jnp.zeros((128 - C, 128), F32)], 0)
    high, low = split(total)
    rest = (total - high.astype(F32) - low.astype(F32)).astype(BF16)
    ones = jnp.ones((sums.shape[0], 128), BF16)
    nt = ((1,), (1,))
    sums[...] = dot(ones, high, nt) + (dot(ones, low, nt) + dot(ones, rest, nt))
    leave.wait()


def call(body, outs, spaces, scratch=(), cost=(0, 0)):
    whole = {"v": pl.BlockSpec(memory_space=pltpu.VMEM), "s": pl.BlockSpec(memory_space=pltpu.SMEM), "h": pl.BlockSpec(memory_space=pltpu.HBM)}
    ins, goals = spaces.split(">")
    return pl.pallas_call(
        body,
        out_shape=[jax.ShapeDtypeStruct(shape, kind) for shape, kind in outs],
        in_specs=[whole[space] for space in ins],
        out_specs=[whole[space] for space in goals],
        scratch_shapes=list(scratch),
        compiler_params=pltpu.CompilerParams(vmem_limit_bytes=VMEM_LIMIT),
        cost_estimate=pl.CostEstimate(flops=cost[0], bytes_accessed=cost[1], transcendentals=0),
    )


def exchange(array, names, size, first):
    order = [[(first + n) % size for n in range(size)]]
    return lax.all_to_all(array, names, 0, 0, axis_index_groups=order, tiled=True)


def hbm(array):
    return pltpu.with_memory_space_constraint(array, pltpu.HBM)


def on_device(sizes, features, target, out_weight, rotation, blocks, wedge):
    slab = tuple(name for name, _ in PARTS["slab"])
    features = features.reshape(C * ROWS, N)
    target = target.reshape(ROWS, N)
    fwd_high, fwd_low, along_high, along_low = [hbm(jnp.asarray(table)) for table in tables()]
    lines, features, fwd_high, fwd_low = call(
        forward_x,
        [((128, 128), F32), ((C * ROWS, N), BF16), (fwd_high.shape, BF16), (fwd_low.shape, BF16)],
        "hhhhh>vvvv",
        [pltpu.SMEM((C,), F32), pltpu.VMEM((ROWS, N), BF16), pltpu.SemaphoreType.DMA((4 + CHUNKS,))],
        (200_000_000, 3_000_000),
    )(hbm(out_weight), hbm(target), hbm(features), fwd_high, fwd_low)
    rotation, lines = lax.optimization_barrier((rotation, lines))
    factors, along_high, along_low = call(
        prepare,
        [((N, 128), F32), (along_high.shape, BF16), (along_low.shape, BF16)],
        "shhhh>vvv",
        [pltpu.SMEM((2, NB), jnp.int32), pltpu.VMEM((N, N), jnp.int32), pltpu.SemaphoreType.DMA((4,))],
        (200_000_000, 3_000_000),
    )(rotation, hbm(blocks.T), hbm(wedge), along_high, along_low)
    lines = exchange(lines.reshape(SLABS, 4, 128), slab, SLABS, HALF).reshape(128, 128)
    (back,) = call(filter_z, [((128, 128), F32)], "vvvv>v", (), (200_000_000, 2_000_000))(
        lines, factors, along_high, along_low
    )
    back = exchange(back.reshape(SLABS, 4, 128), slab, SLABS, HALF).reshape(128, 128)
    far = math.prod(sizes[name] for name in FAR)
    near = math.prod(sizes[name] for name in NEAR)
    volume, sums = call(
        inverse_x,
        [((ROWS, N), F32), ((far, 128), F32)],
        "vvvv>hv",
        [pltpu.VMEM((ROWS, N), F32), pltpu.VMEM((C * YP, 128), F32), pltpu.SemaphoreType.DMA],
        (200_000_000, 3_000_000),
    )(back, features, fwd_high, fwd_low)
    sums = exchange(sums.reshape(far, 1, 128), FAR, far, FIRST_FAR % far)
    sums = jnp.sum(sums, 0, keepdims=True)
    sums = jnp.broadcast_to(sums, (near, 1, 128))
    sums = exchange(sums, NEAR, near, FIRST_NEAR % near)
    w_grad = jnp.sum(sums, (0, 1))[:C] * (1.0 / (math.prod(sizes.values()) * ROWS * N))
    return volume.reshape(1, ZL, YP, N), w_grad


def solution(mesh):
    parts = PARTS["dp"] + PARTS["slab"]
    sizes = dict(parts)
    dp = tuple(name for name, _ in PARTS["dp"])
    slab = tuple(name for name, _ in PARTS["slab"])
    fine = Mesh(mesh.devices.reshape([size for _, size in parts]), tuple(sizes))
    in_specs = (P(dp, None, slab, None, None), P(dp, slab, None, None), P(), P(dp), P(), P())
    out_specs = (P(dp, slab, None, None), P())
    return jax.shard_map(
        functools.partial(on_device, sizes), mesh=fine, in_specs=in_specs, out_specs=out_specs, check_vma=False
    )
```

```python
import functools
import math

import jax
import jax.numpy as jnp
import numpy as np
from jax import lax
from jax.experimental import pallas as pl
from jax.experimental.pallas import tpu as pltpu
from jax.sharding import Mesh
from jax.sharding import PartitionSpec as P

N = 256
C = 64
BLK = 64
NB = 8
SLABS = 32
ZL = 8
YP = 8
ROWS = ZL * YP
CHUNKS = 8
PARTS = {"dp": (("y", 4), ("xh", 2), ("core", 2)), "slab": (("z", 16), ("xl", 2))}
NEAR = ("y", "xh", "xl")
FAR = ("core", "z")
HALF = SLABS // 2
FIRST_FAR = 24
FIRST_NEAR = 10

F32, BF16 = jnp.float32, jnp.bfloat16
VMEM_LIMIT = 16 * 1024 * 1024


def halves(table):
    high = table.astype(np.float32).astype(BF16)
    low = (table - high.astype(np.float64)).astype(np.float32).astype(BF16)
    return high, low


def tables():
    step = 2.0 * math.pi / N
    space = np.arange(N)
    quad, slab = np.meshgrid(np.arange(4), np.arange(SLABS), indexing="ij")
    freq = (4 * ((slab + HALF) % SLABS) + quad).reshape(-1)
    phase = (freq[:, None] * space[None, :]) % N * step
    real, imag = np.cos(phase), -np.sin(phase)
    imag[freq == 0] = np.cos(math.pi * space)
    zp, m, i = np.meshgrid(np.arange(2), np.arange(4), np.arange(SLABS), indexing="ij")
    depth = (8 * ((i + HALF) % SLABS) + 2 * m + zp).reshape(-1)
    phase = (depth[:, None] * depth[None, :]) % N * step
    along = np.concatenate([np.cos(phase), np.sin(phase)], 0)
    return halves(np.concatenate([real, imag], 0)) + halves(along)


def split(values):
    high = values.astype(BF16)
    return high, (values - high.astype(F32)).astype(BF16)


def dot(left, right, dims=((1,), (0,))):
    return lax.dot_general(left, right, (dims, ((), ())), preferred_element_type=F32)


def lane_of(shape):
    return lax.broadcasted_iota(jnp.int32, shape, 1)


def regroup(pieces, to):
    group = (lane_of(pieces[0].shape) >> 4) & 3
    result = None
    for source in range(4):
        moved = pieces[source] if source == to else pltpu.roll(pieces[source], (16 * (source - to)) % 128, 1)
        result = moved if result is None else jnp.where(group == source, moved, result)
    return result


def slab_index():
    return lax.axis_index(tuple(name for name, _ in PARTS["slab"])).astype(jnp.int32)


def filter_weights(turn, place, blocks, wedge, out):
    kz = lax.broadcasted_iota(jnp.int32, (8, N), 0)
    kx = lane_of((8, N)) >> 6
    listed = jnp.zeros((8, N), jnp.bool_)
    for n in range(NB):
        listed = listed | ((kz == blocks[0, n]) & (kx == blocks[1, n]))
    listed = listed.astype(F32)
    mask = jnp.concatenate(
        [wedge[a * BLK : (a + 1) * BLK, :].astype(F32) * listed[a : a + 1, :] for a in range(N // BLK)], 0
    ).astype(BF16)
    lane = lane_of((N, 128))
    row = lax.broadcasted_iota(jnp.int32, (N, 128), 0)
    quad = (lane >> 4) & 3
    freq = 4 * place + quad
    freq = jnp.where((freq == 0) & (lane >= 64), N // 2, freq)
    plus = (row == freq).astype(F32).astype(BF16)
    minus = (row == ((N - freq) & (N - 1))).astype(F32).astype(BF16)
    picks = jnp.concatenate([plus, minus], 1)
    odd = (turn & 1) == 1
    plain = dot(mask, picks)
    other = dot(mask, picks, ((0,), (0,)))
    direct = jnp.where(odd, other[:, 128:], plain[:, :128])
    mirror = jnp.where(odd, other[:, :128], plain[:, 128:]).astype(BF16)
    r = lax.broadcasted_iota(jnp.int32, (N, N), 0)
    p = (8 * ((r & 31) + HALF) + 2 * ((r >> 5) & 3) + (r >> 7)) & (N - 1)
    k = lane_of((N, N))
    keep = (k == p).astype(F32).astype(BF16)
    flip = (((p + k) & (N - 1)) == 0).astype(F32).astype(BF16)
    out[...] = dot(keep, direct.astype(BF16)) + dot(flip, mirror)


def prepare(turn, blocks_hbm, wedge_hbm, high_hbm, low_hbm, factors, high, low, blocks, wedge, sems):
    pairs = [(blocks_hbm, blocks), (wedge_hbm, wedge), (high_hbm, high), (low_hbm, low)]
    copies = [pltpu.make_async_copy(source, goal, sems.at[n]) for n, (source, goal) in enumerate(pairs)]
    for copy in copies:
        copy.start()
    for copy in copies[:2]:
        copy.wait()
    filter_weights(turn[0], slab_index(), blocks, wedge, factors)
    for copy in copies[2:]:
        copy.wait()


def forward_x(weight_hbm, target_hbm, features_hbm, high_hbm, low_hbm, lines, features, fwd_high, fwd_low, weight, target, sems):
    part = C * ROWS // CHUNKS
    pairs = [(weight_hbm, weight), (target_hbm, target)]
    for k in range(CHUNKS):
        rows = pl.ds(k * part, part)
        pairs.append((features_hbm.at[rows], features.at[rows]))
    pairs += [(high_hbm, fwd_high), (low_hbm, fwd_low)]
    copies = [pltpu.make_async_copy(source, goal, sems.at[n]) for n, (source, goal) in enumerate(pairs)]
    for copy in copies:
        copy.start()
    for copy in copies[:2]:
        copy.wait()
    total = -target[...].astype(F32)
    for k in range(CHUNKS):
        copies[2 + k].wait()
        for c in range(k * C // CHUNKS, (k + 1) * C // CHUNKS):
            total = total + weight[c] * features[c * ROWS : (c + 1) * ROWS, :].astype(F32)
    high, low = split(total)
    nt = ((1,), (1,))
    for copy in copies[2 + CHUNKS :]:
        copy.wait()
    both = dot(fwd_high[...], jnp.concatenate([high, low], 0), nt)
    line = dot(fwd_low[...], jnp.concatenate([high, high], 0), nt) + (both + pltpu.roll(both, 64, 1))
    line = jnp.where(lane_of((128, 128)) < 64, line[:128], line[128:])
    pieces = [line[q * SLABS : (q + 1) * SLABS] for q in range(4)]
    for m in range(4):
        lines[pl.ds(m, SLABS, stride=4), :] = regroup(pieces, m)


def three(left_high, left_low, right):
    high, low = split(right)
    both = dot(left_high, jnp.concatenate([high, low], 1))
    return dot(left_low, high) + (both[:, :128] + both[:, 128:])


def filter_z(lines, factors, along_high, along_low, back):
    even = jnp.concatenate([lines[pl.ds(m, SLABS, stride=4), :] for m in range(4)], 0)
    data = jnp.concatenate([even, pltpu.roll(even, 120, 1)], 0)
    freq = three(along_high[...], along_low[...], data)
    cosine, sine = freq[:N], freq[N:]
    lane = lane_of((N, 128))
    sign = jnp.where(lane < 64, 1.0, -1.0)
    sign = jnp.where((slab_index() == 0) & (((lane >> 4) & 3) == 0), 0.0, sign)
    scale = factors[...]
    kept_cosine = scale * (cosine + sign * pltpu.roll(sine, 64, 1))
    kept_sine = scale * (sine - sign * pltpu.roll(cosine, 64, 1))
    depth = three(along_high[:N, :], along_low[:N, :], kept_cosine) + three(along_high[N:, :], along_low[N:, :], kept_sine)
    lane = lane_of((SLABS, 128))
    for m in range(4):
        first = depth[m * SLABS : (m + 1) * SLABS]
        second = depth[128 + m * SLABS : 128 + (m + 1) * SLABS]
        back[pl.ds(m, SLABS, stride=4), :] = jnp.where((lane & 8) == 0, first, pltpu.roll(second, 8, 1))


def inverse_x(lines, features, fwd_high, fwd_low, volume, sums, result, partial, sem):
    blocks = [lines[pl.ds(m, SLABS, stride=4), :] for m in range(4)]
    line = jnp.concatenate([regroup(blocks, q) for q in range(4)], 0).T
    line = jnp.concatenate([line[:64], line[64:]], 1)
    line = line * jnp.where((lane_of((ROWS, N)) & 127) == HALF, 1.0 / (N * N), 2.0 / (N * N))
    high, low = split(line)
    both = dot(jnp.concatenate([high, low], 0), fwd_high[...])
    values = both[:ROWS] + (both[ROWS:] + dot(high, fwd_low[...]))
    result[...] = values
    leave = pltpu.make_async_copy(result, volume, sem)
    leave.start()

    def channels(step, carry):
        for k in range(8):
            c = step * 8 + k
            piece = features[pl.ds(pl.multiple_of(c * ROWS, ROWS), ROWS), :].astype(F32) * values
            piece = sum(piece[z * YP : (z + 1) * YP] for z in range(ZL))
            partial[pl.ds(pl.multiple_of(c * YP, YP), YP), :] = piece[:, :128] + piece[:, 128:]
        return carry

    lax.fori_loop(0, C // 8, channels, 0)
    total = sum(partial[pl.ds(y, C, stride=YP), :] for y in range(YP))
    total = jnp.concatenate([total, jnp.zeros((128 - C, 128), F32)], 0)
    high, low = split(total)
    rest = (total - high.astype(F32) - low.astype(F32)).astype(BF16)
    ones = jnp.ones((sums.shape[0], 128), BF16)
    nt = ((1,), (1,))
    sums[...] = dot(ones, high, nt) + (dot(ones, low, nt) + dot(ones, rest, nt))
    leave.wait()


def call(body, outs, spaces, scratch=(), cost=(0, 0)):
    whole = {"v": pl.BlockSpec(memory_space=pltpu.VMEM), "s": pl.BlockSpec(memory_space=pltpu.SMEM), "h": pl.BlockSpec(memory_space=pltpu.HBM)}
    ins, goals = spaces.split(">")
    return pl.pallas_call(
        body,
        out_shape=[jax.ShapeDtypeStruct(shape, kind) for shape, kind in outs],
        in_specs=[whole[space] for space in ins],
        out_specs=[whole[space] for space in goals],
        scratch_shapes=list(scratch),
        compiler_params=pltpu.CompilerParams(vmem_limit_bytes=VMEM_LIMIT),
        cost_estimate=pl.CostEstimate(flops=cost[0], bytes_accessed=cost[1], transcendentals=0),
    )


def exchange(array, names, size, first):
    order = [[(first + n) % size for n in range(size)]]
    return lax.all_to_all(array, names, 0, 0, axis_index_groups=order, tiled=True)


def hbm(array):
    return pltpu.with_memory_space_constraint(array, pltpu.HBM)


def on_device(sizes, features, target, out_weight, rotation, blocks, wedge):
    slab = tuple(name for name, _ in PARTS["slab"])
    features = features.reshape(C * ROWS, N)
    target = target.reshape(ROWS, N)
    fwd_high, fwd_low, along_high, along_low = [hbm(jnp.asarray(table)) for table in tables()]
    lines, features, fwd_high, fwd_low = call(
        forward_x,
        [((128, 128), F32), ((C * ROWS, N), BF16), (fwd_high.shape, BF16), (fwd_low.shape, BF16)],
        "hhhhh>vvvv",
        [pltpu.SMEM((C,), F32), pltpu.VMEM((ROWS, N), BF16), pltpu.SemaphoreType.DMA((4 + CHUNKS,))],
        (200_000_000, 3_000_000),
    )(hbm(out_weight), hbm(target), hbm(features), fwd_high, fwd_low)
    rotation, lines = lax.optimization_barrier((rotation, lines))
    factors, along_high, along_low = call(
        prepare,
        [((N, 128), F32), (along_high.shape, BF16), (along_low.shape, BF16)],
        "shhhh>vvv",
        [pltpu.SMEM((2, NB), jnp.int32), pltpu.VMEM((N, N), jnp.int32), pltpu.SemaphoreType.DMA((4,))],
        (200_000_000, 3_000_000),
    )(rotation, hbm(blocks.T), hbm(wedge), along_high, along_low)
    lines = exchange(lines.reshape(SLABS, 4, 128), slab, SLABS, HALF).reshape(128, 128)
    (back,) = call(filter_z, [((128, 128), F32)], "vvvv>v", (), (200_000_000, 2_000_000))(
        lines, factors, along_high, along_low
    )
    back = exchange(back.reshape(SLABS, 4, 128), slab, SLABS, HALF).reshape(128, 128)
    far = math.prod(sizes[name] for name in FAR)
    near = math.prod(sizes[name] for name in NEAR)
    volume, sums = call(
        inverse_x,
        [((ROWS, N), F32), ((far, 128), F32)],
        "vvvv>hv",
        [pltpu.VMEM((ROWS, N), F32), pltpu.VMEM((C * YP, 128), F32), pltpu.SemaphoreType.DMA],
        (200_000_000, 3_000_000),
    )(back, features, fwd_high, fwd_low)
    sums = exchange(sums.reshape(far, 1, 128), FAR, far, FIRST_FAR % far)
    sums = jnp.sum(sums, 0, keepdims=True)
    sums = jnp.broadcast_to(sums, (near, 1, 128))
    sums = exchange(sums, NEAR, near, FIRST_NEAR % near)
    w_grad = jnp.sum(sums, (0, 1))[:C] * (1.0 / (math.prod(sizes.values()) * ROWS * N))
    return volume.reshape(1, ZL, YP, N), w_grad


def solution(mesh):
    parts = PARTS["dp"] + PARTS["slab"]
    sizes = dict(parts)
    dp = tuple(name for name, _ in PARTS["dp"])
    slab = tuple(name for name, _ in PARTS["slab"])
    fine = Mesh(mesh.devices.reshape([size for _, size in parts]), tuple(sizes))
    in_specs = (P(dp, None, slab, None, None), P(dp, slab, None, None), P(), P(dp), P(), P())
    out_specs = (P(dp, slab, None, None), P())
    return jax.shard_map(
        functools.partial(on_device, sizes), mesh=fine, in_specs=in_specs, out_specs=out_specs, check_vma=False
    )
```

```python
import functools
import math

import jax
import jax.numpy as jnp
import numpy as np
from jax import lax
from jax.experimental import pallas as pl
from jax.experimental.pallas import tpu as pltpu
from jax.sharding import Mesh
from jax.sharding import PartitionSpec as P

N = 256
C = 64
BLK = 64
NB = 8
SLABS = 32
ZL = 8
YP = 8
ROWS = ZL * YP
CHUNKS = 8
PARTS = {"dp": (("y", 4), ("xh", 2), ("core", 2)), "slab": (("z", 16), ("xl", 2))}
NEAR = ("y", "xh", "xl")
FAR = ("core", "z")
HALF = SLABS // 2
FIRST_FAR = 24
FIRST_NEAR = 10

F32, BF16 = jnp.float32, jnp.bfloat16
VMEM_LIMIT = 16 * 1024 * 1024


def halves(table):
    high = table.astype(np.float32).astype(BF16)
    low = (table - high.astype(np.float64)).astype(np.float32).astype(BF16)
    return high, low


def tables():
    step = 2.0 * math.pi / N
    space = np.arange(N)
    quad, slab = np.meshgrid(np.arange(4), np.arange(SLABS), indexing="ij")
    freq = (4 * ((slab + HALF) % SLABS) + quad).reshape(-1)
    phase = (freq[:, None] * space[None, :]) % N * step
    real, imag = np.cos(phase), -np.sin(phase)
    imag[freq == 0] = np.cos(math.pi * space)
    zp, m, i = np.meshgrid(np.arange(2), np.arange(4), np.arange(SLABS), indexing="ij")
    depth = (8 * ((i + HALF) % SLABS) + 2 * m + zp).reshape(-1)
    phase = (depth[:, None] * depth[None, :]) % N * step
    along = np.concatenate([np.cos(phase), np.sin(phase)], 0)
    return halves(np.concatenate([real, imag], 0)) + halves(along)


def split(values):
    high = values.astype(BF16)
    return high, (values - high.astype(F32)).astype(BF16)


def dot(left, right, dims=((1,), (0,))):
    return lax.dot_general(left, right, (dims, ((), ())), preferred_element_type=F32)


def lane_of(shape):
    return lax.broadcasted_iota(jnp.int32, shape, 1)


def regroup(pieces, to):
    group = (lane_of(pieces[0].shape) >> 4) & 3
    result = None
    for source in range(4):
        moved = pieces[source] if source == to else pltpu.roll(pieces[source], (16 * (source - to)) % 128, 1)
        result = moved if result is None else jnp.where(group == source, moved, result)
    return result


def slab_index():
    return lax.axis_index(tuple(name for name, _ in PARTS["slab"])).astype(jnp.int32)


def filter_weights(turn, place, blocks, wedge, out):
    kz = lax.broadcasted_iota(jnp.int32, (8, N), 0)
    kx = lane_of((8, N)) >> 6
    listed = jnp.zeros((8, N), jnp.bool_)
    for n in range(NB):
        listed = listed | ((kz == blocks[0, n]) & (kx == blocks[1, n]))
    listed = listed.astype(F32)
    mask = jnp.concatenate(
        [wedge[a * BLK : (a + 1) * BLK, :].astype(F32) * listed[a : a + 1, :] for a in range(N // BLK)], 0
    ).astype(BF16)
    lane = lane_of((N, 128))
    row = lax.broadcasted_iota(jnp.int32, (N, 128), 0)
    quad = (lane >> 4) & 3
    freq = 4 * place + quad
    freq = jnp.where((freq == 0) & (lane >= 64), N // 2, freq)
    plus = (row == freq).astype(F32).astype(BF16)
    minus = (row == ((N - freq) & (N - 1))).astype(F32).astype(BF16)
    picks = jnp.concatenate([plus, minus], 1)
    odd = (turn & 1) == 1
    plain = dot(mask, picks)
    other = dot(mask, picks, ((0,), (0,)))
    direct = jnp.where(odd, other[:, 128:], plain[:, :128])
    mirror = jnp.where(odd, other[:, :128], plain[:, 128:]).astype(BF16)
    r = lax.broadcasted_iota(jnp.int32, (N, N), 0)
    p = (8 * ((r & 31) + HALF) + 2 * ((r >> 5) & 3) + (r >> 7)) & (N - 1)
    k = lane_of((N, N))
    keep = (k == p).astype(F32).astype(BF16)
    flip = (((p + k) & (N - 1)) == 0).astype(F32).astype(BF16)
    out[...] = dot(keep, direct.astype(BF16)) + dot(flip, mirror)


def prepare(turn, blocks_hbm, wedge_hbm, high_hbm, low_hbm, factors, high, low, blocks, wedge, sems):
    pairs = [(blocks_hbm, blocks), (wedge_hbm, wedge), (high_hbm, high), (low_hbm, low)]
    copies = [pltpu.make_async_copy(source, goal, sems.at[n]) for n, (source, goal) in enumerate(pairs)]
    for copy in copies:
        copy.start()
    for copy in copies[:2]:
        copy.wait()
    filter_weights(turn[0], slab_index(), blocks, wedge, factors)
    for copy in copies[2:]:
        copy.wait()


def forward_x(weight_hbm, target_hbm, features_hbm, high_hbm, low_hbm, lines, features, fwd_high, fwd_low, weight, target, sems):
    part = C * ROWS // CHUNKS
    pairs = [(weight_hbm, weight), (target_hbm, target)]
    for k in range(CHUNKS):
        rows = pl.ds(k * part, part)
        pairs.append((features_hbm.at[rows], features.at[rows]))
    pairs += [(high_hbm, fwd_high), (low_hbm, fwd_low)]
    copies = [pltpu.make_async_copy(source, goal, sems.at[n]) for n, (source, goal) in enumerate(pairs)]
    for copy in copies:
        copy.start()
    for copy in copies[:2]:
        copy.wait()
    total = -target[...].astype(F32)
    for k in range(CHUNKS):
        copies[2 + k].wait()
        for c in range(k * C // CHUNKS, (k + 1) * C // CHUNKS):
            total = total + weight[c] * features[c * ROWS : (c + 1) * ROWS, :].astype(F32)
    high, low = split(total)
    nt = ((1,), (1,))
    for copy in copies[2 + CHUNKS :]:
        copy.wait()
    both = dot(fwd_high[...], jnp.concatenate([high, low], 0), nt)
    line = dot(fwd_low[...], jnp.concatenate([high, high], 0), nt) + (both + pltpu.roll(both, 64, 1))
    line = jnp.where(lane_of((128, 128)) < 64, line[:128], line[128:])
    pieces = [line[q * SLABS : (q + 1) * SLABS] for q in range(4)]
    for m in range(4):
        lines[pl.ds(m, SLABS, stride=4), :] = regroup(pieces, m)


def three(left_high, left_low, right):
    high, low = split(right)
    both = dot(left_high, jnp.concatenate([high, low], 1))
    return dot(left_low, high) + (both[:, :128] + both[:, 128:])


def filter_z(lines, factors, along_high, along_low, back):
    even = jnp.concatenate([lines[pl.ds(m, SLABS, stride=4), :] for m in range(4)], 0)
    data = jnp.concatenate([even, pltpu.roll(even, 120, 1)], 0)
    freq = three(along_high[...], along_low[...], data)
    cosine, sine = freq[:N], freq[N:]
    lane = lane_of((N, 128))
    sign = jnp.where(lane < 64, 1.0, -1.0)
    sign = jnp.where((slab_index() == 0) & (((lane >> 4) & 3) == 0), 0.0, sign)
    scale = factors[...]
    kept_cosine = scale * (cosine + sign * pltpu.roll(sine, 64, 1))
    kept_sine = scale * (sine - sign * pltpu.roll(cosine, 64, 1))
    depth = three(along_high[:N, :], along_low[:N, :], kept_cosine) + three(along_high[N:, :], along_low[N:, :], kept_sine)
    lane = lane_of((SLABS, 128))
    for m in range(4):
        first = depth[m * SLABS : (m + 1) * SLABS]
        second = depth[128 + m * SLABS : 128 + (m + 1) * SLABS]
        back[pl.ds(m, SLABS, stride=4), :] = jnp.where((lane & 8) == 0, first, pltpu.roll(second, 8, 1))


def inverse_x(lines, features, fwd_high, fwd_low, volume, sums, result, partial, sem):
    blocks = [lines[pl.ds(m, SLABS, stride=4), :] for m in range(4)]
    line = jnp.concatenate([regroup(blocks, q) for q in range(4)], 0).T
    line = jnp.concatenate([line[:64], line[64:]], 1)
    line = line * jnp.where((lane_of((ROWS, N)) & 127) == HALF, 1.0 / (N * N), 2.0 / (N * N))
    high, low = split(line)
    both = dot(jnp.concatenate([high, low], 0), fwd_high[...])
    values = both[:ROWS] + (both[ROWS:] + dot(high, fwd_low[...]))
    result[...] = values
    leave = pltpu.make_async_copy(result, volume, sem)
    leave.start()

    def channels(step, carry):
        for k in range(8):
            c = step * 8 + k
            piece = features[pl.ds(pl.multiple_of(c * ROWS, ROWS), ROWS), :].astype(F32) * values
            piece = sum(piece[z * YP : (z + 1) * YP] for z in range(ZL))
            partial[pl.ds(pl.multiple_of(c * YP, YP), YP), :] = piece[:, :128] + piece[:, 128:]
        return carry

    lax.fori_loop(0, C // 8, channels, 0)
    total = sum(partial[pl.ds(y, C, stride=YP), :] for y in range(YP))
    total = jnp.concatenate([total, jnp.zeros((128 - C, 128), F32)], 0)
    high, low = split(total)
    rest = (total - high.astype(F32) - low.astype(F32)).astype(BF16)
    ones = jnp.ones((sums.shape[0], 128), BF16)
    nt = ((1,), (1,))
    sums[...] = dot(ones, high, nt) + (dot(ones, low, nt) + dot(ones, rest, nt))
    leave.wait()


def call(body, outs, spaces, scratch=(), cost=(0, 0)):
    whole = {"v": pl.BlockSpec(memory_space=pltpu.VMEM), "s": pl.BlockSpec(memory_space=pltpu.SMEM), "h": pl.BlockSpec(memory_space=pltpu.HBM)}
    ins, goals = spaces.split(">")
    return pl.pallas_call(
        body,
        out_shape=[jax.ShapeDtypeStruct(shape, kind) for shape, kind in outs],
        in_specs=[whole[space] for space in ins],
        out_specs=[whole[space] for space in goals],
        scratch_shapes=list(scratch),
        compiler_params=pltpu.CompilerParams(vmem_limit_bytes=VMEM_LIMIT),
        cost_estimate=pl.CostEstimate(flops=cost[0], bytes_accessed=cost[1], transcendentals=0),
    )


def turned_order(size, first):
    return [(first + n) % size for n in range(size)]


def far_first(names, sizes, first):
    dims = [sizes[name] for name in names]
    spots = np.stack(np.unravel_index(np.arange(math.prod(dims)), dims), 1)
    apart = np.abs(spots - spots[first])
    apart = np.minimum(apart, np.array(dims) - apart).sum(1)
    apart[first] = sum(dims)
    return [int(n) for n in np.argsort(-apart, kind="stable")]


def exchange(array, names, order):
    return lax.all_to_all(array, names, 0, 0, axis_index_groups=[order], tiled=True)


def hbm(array):
    return pltpu.with_memory_space_constraint(array, pltpu.HBM)


def on_device(sizes, features, target, out_weight, rotation, blocks, wedge):
    slab = tuple(name for name, _ in PARTS["slab"])
    features = features.reshape(C * ROWS, N)
    target = target.reshape(ROWS, N)
    fwd_high, fwd_low, along_high, along_low = [hbm(jnp.asarray(table)) for table in tables()]
    lines, features, fwd_high, fwd_low = call(
        forward_x,
        [((128, 128), F32), ((C * ROWS, N), BF16), (fwd_high.shape, BF16), (fwd_low.shape, BF16)],
        "hhhhh>vvvv",
        [pltpu.SMEM((C,), F32), pltpu.VMEM((ROWS, N), BF16), pltpu.SemaphoreType.DMA((4 + CHUNKS,))],
        (200_000_000, 3_000_000),
    )(hbm(out_weight), hbm(target), hbm(features), fwd_high, fwd_low)
    rotation, lines = lax.optimization_barrier((rotation, lines))
    factors, along_high, along_low = call(
        prepare,
        [((N, 128), F32), (along_high.shape, BF16), (along_low.shape, BF16)],
        "shhhh>vvv",
        [pltpu.SMEM((2, NB), jnp.int32), pltpu.VMEM((N, N), jnp.int32), pltpu.SemaphoreType.DMA((4,))],
        (200_000_000, 3_000_000),
    )(rotation, hbm(blocks.T), hbm(wedge), along_high, along_low)
    lines = exchange(lines.reshape(SLABS, 4, 128), slab, turned_order(SLABS, HALF)).reshape(128, 128)
    (back,) = call(filter_z, [((128, 128), F32)], "vvvv>v", (), (200_000_000, 2_000_000))(
        lines, factors, along_high, along_low
    )
    back = exchange(back.reshape(SLABS, 4, 128), slab, turned_order(SLABS, HALF)).reshape(128, 128)
    far = math.prod(sizes[name] for name in FAR)
    near = math.prod(sizes[name] for name in NEAR)
    volume, sums = call(
        inverse_x,
        [((ROWS, N), F32), ((far, 128), F32)],
        "vvvv>hv",
        [pltpu.VMEM((ROWS, N), F32), pltpu.VMEM((C * YP, 128), F32), pltpu.SemaphoreType.DMA],
        (200_000_000, 3_000_000),
    )(back, features, fwd_high, fwd_low)
    sums = exchange(sums.reshape(far, 1, 128), FAR, far_first(FAR, sizes, FIRST_FAR % far))
    sums = jnp.sum(sums, 0, keepdims=True)
    sums = jnp.broadcast_to(sums, (near, 1, 128))
    sums = exchange(sums, NEAR, far_first(NEAR, sizes, FIRST_NEAR % near))
    w_grad = jnp.sum(sums, (0, 1))[:C] * (1.0 / (math.prod(sizes.values()) * ROWS * N))
    return volume.reshape(1, ZL, YP, N), w_grad


def solution(mesh):
    parts = PARTS["dp"] + PARTS["slab"]
    sizes = dict(parts)
    dp = tuple(name for name, _ in PARTS["dp"])
    slab = tuple(name for name, _ in PARTS["slab"])
    fine = Mesh(mesh.devices.reshape([size for _, size in parts]), tuple(sizes))
    in_specs = (P(dp, None, slab, None, None), P(dp, slab, None, None), P(), P(dp), P(), P())
    out_specs = (P(dp, slab, None, None), P())
    return jax.shard_map(
        functools.partial(on_device, sizes), mesh=fine, in_specs=in_specs, out_specs=out_specs, check_vma=False
    )
```

```python
import functools
import math

import jax
import jax.numpy as jnp
import numpy as np
from jax import lax
from jax.experimental import pallas as pl
from jax.experimental.pallas import tpu as pltpu
from jax.sharding import Mesh
from jax.sharding import PartitionSpec as P

N = 256
C = 64
BLK = 64
NB = 8
SLABS = 32
ZL = 8
YP = 8
ROWS = ZL * YP
CHUNKS = 8
PARTS = {"dp": (("y", 4), ("xh", 2), ("core", 2)), "slab": (("z", 16), ("xl", 2))}
NEAR = ("y", "xh", "xl")
FAR = ("core", "z")
TURN = SLABS // 2 + 1
FIRST_FAR = 24
FIRST_NEAR = 10

F32, BF16 = jnp.float32, jnp.bfloat16
VMEM_LIMIT = 16 * 1024 * 1024


def halves(table):
    high = table.astype(np.float32).astype(BF16)
    low = (table - high.astype(np.float64)).astype(np.float32).astype(BF16)
    return high, low


def tables():
    step = 2.0 * math.pi / N
    space = np.arange(N)
    quad, slab = np.meshgrid(np.arange(4), np.arange(SLABS), indexing="ij")
    freq = (4 * ((slab + TURN) % SLABS) + quad).reshape(-1)
    phase = (freq[:, None] * space[None, :]) % N * step
    real, imag = np.cos(phase), -np.sin(phase)
    imag[freq == 0] = np.cos(math.pi * space)
    zp, m, i = np.meshgrid(np.arange(2), np.arange(4), np.arange(SLABS), indexing="ij")
    depth = (8 * ((i + TURN) % SLABS) + 2 * m + zp).reshape(-1)
    phase = (depth[:, None] * depth[None, :]) % N * step
    along = np.concatenate([np.cos(phase), np.sin(phase)], 0)
    return halves(np.concatenate([real, imag], 0)) + halves(along)


def split(values):
    high = values.astype(BF16)
    return high, (values - high.astype(F32)).astype(BF16)


def dot(left, right, dims=((1,), (0,))):
    return lax.dot_general(left, right, (dims, ((), ())), preferred_element_type=F32)


def lane_of(shape):
    return lax.broadcasted_iota(jnp.int32, shape, 1)


def regroup(pieces, to):
    group = (lane_of(pieces[0].shape) >> 4) & 3
    result = None
    for source in range(4):
        moved = pieces[source] if source == to else pltpu.roll(pieces[source], (16 * (source - to)) % 128, 1)
        result = moved if result is None else jnp.where(group == source, moved, result)
    return result


def slab_index():
    return lax.axis_index(tuple(name for name, _ in PARTS["slab"])).astype(jnp.int32)


def filter_weights(turn, place, blocks, wedge, out):
    kz = lax.broadcasted_iota(jnp.int32, (8, N), 0)
    kx = lane_of((8, N)) >> 6
    listed = jnp.zeros((8, N), jnp.bool_)
    for n in range(NB):
        listed = listed | ((kz == blocks[0, n]) & (kx == blocks[1, n]))
    listed = listed.astype(F32)
    mask = jnp.concatenate(
        [wedge[a * BLK : (a + 1) * BLK, :].astype(F32) * listed[a : a + 1, :] for a in range(N // BLK)], 0
    ).astype(BF16)
    lane = lane_of((N, 128))
    row = lax.broadcasted_iota(jnp.int32, (N, 128), 0)
    quad = (lane >> 4) & 3
    freq = 4 * place + quad
    freq = jnp.where((freq == 0) & (lane >= 64), N // 2, freq)
    plus = (row == freq).astype(F32).astype(BF16)
    minus = (row == ((N - freq) & (N - 1))).astype(F32).astype(BF16)
    picks = jnp.concatenate([plus, minus], 1)
    odd = (turn & 1) == 1
    plain = dot(mask, picks)
    other = dot(mask, picks, ((0,), (0,)))
    direct = jnp.where(odd, other[:, 128:], plain[:, :128])
    mirror = jnp.where(odd, other[:, :128], plain[:, 128:]).astype(BF16)
    r = lax.broadcasted_iota(jnp.int32, (N, N), 0)
    p = (8 * ((r & 31) + TURN) + 2 * ((r >> 5) & 3) + (r >> 7)) & (N - 1)
    k = lane_of((N, N))
    keep = (k == p).astype(F32).astype(BF16)
    flip = (((p + k) & (N - 1)) == 0).astype(F32).astype(BF16)
    out[...] = dot(keep, direct.astype(BF16)) + dot(flip, mirror)


def prepare(turn, blocks_hbm, wedge_hbm, high_hbm, low_hbm, factors, high, low, blocks, wedge, sems):
    pairs = [(blocks_hbm, blocks), (wedge_hbm, wedge), (high_hbm, high), (low_hbm, low)]
    copies = [pltpu.make_async_copy(source, goal, sems.at[n]) for n, (source, goal) in enumerate(pairs)]
    for copy in copies:
        copy.start()
    for copy in copies[:2]:
        copy.wait()
    filter_weights(turn[0], slab_index(), blocks, wedge, factors)
    for copy in copies[2:]:
        copy.wait()


def forward_x(weight_hbm, target_hbm, features_hbm, high_hbm, low_hbm, lines, features, fwd_high, fwd_low, weight, target, sems):
    part = C * ROWS // CHUNKS
    pairs = [(weight_hbm, weight), (target_hbm, target)]
    for k in range(CHUNKS):
        rows = pl.ds(k * part, part)
        pairs.append((features_hbm.at[rows], features.at[rows]))
    pairs += [(high_hbm, fwd_high), (low_hbm, fwd_low)]
    copies = [pltpu.make_async_copy(source, goal, sems.at[n]) for n, (source, goal) in enumerate(pairs)]
    for copy in copies:
        copy.start()
    for copy in copies[:2]:
        copy.wait()
    total = -target[...].astype(F32)
    for k in range(CHUNKS):
        copies[2 + k].wait()
        for c in range(k * C // CHUNKS, (k + 1) * C // CHUNKS):
            total = total + weight[c] * features[c * ROWS : (c + 1) * ROWS, :].astype(F32)
    high, low = split(total)
    nt = ((1,), (1,))
    for copy in copies[2 + CHUNKS :]:
        copy.wait()
    both = dot(fwd_high[...], jnp.concatenate([high, low], 0), nt)
    line = dot(fwd_low[...], jnp.concatenate([high, high], 0), nt) + (both + pltpu.roll(both, 64, 1))
    line = jnp.where(lane_of((128, 128)) < 64, line[:128], line[128:])
    pieces = [line[q * SLABS : (q + 1) * SLABS] for q in range(4)]
    for m in range(4):
        lines[pl.ds(m, SLABS, stride=4), :] = regroup(pieces, m)


def three(left_high, left_low, right):
    high, low = split(right)
    both = dot(left_high, jnp.concatenate([high, low], 1))
    return dot(left_low, high) + (both[:, :128] + both[:, 128:])


def filter_z(lines, factors, along_high, along_low, back):
    even = jnp.concatenate([lines[pl.ds(m, SLABS, stride=4), :] for m in range(4)], 0)
    data = jnp.concatenate([even, pltpu.roll(even, 120, 1)], 0)
    freq = three(along_high[...], along_low[...], data)
    cosine, sine = freq[:N], freq[N:]
    lane = lane_of((N, 128))
    sign = jnp.where(lane < 64, 1.0, -1.0)
    sign = jnp.where((slab_index() == 0) & (((lane >> 4) & 3) == 0), 0.0, sign)
    scale = factors[...]
    kept_cosine = scale * (cosine + sign * pltpu.roll(sine, 64, 1))
    kept_sine = scale * (sine - sign * pltpu.roll(cosine, 64, 1))
    depth = three(along_high[:N, :], along_low[:N, :], kept_cosine) + three(along_high[N:, :], along_low[N:, :], kept_sine)
    lane = lane_of((SLABS, 128))
    for m in range(4):
        first = depth[m * SLABS : (m + 1) * SLABS]
        second = depth[128 + m * SLABS : 128 + (m + 1) * SLABS]
        back[pl.ds(m, SLABS, stride=4), :] = jnp.where((lane & 8) == 0, first, pltpu.roll(second, 8, 1))


def inverse_x(lines, features, fwd_high, fwd_low, volume, sums, result, partial, sem):
    blocks = [lines[pl.ds(m, SLABS, stride=4), :] for m in range(4)]
    line = jnp.concatenate([regroup(blocks, q) for q in range(4)], 0).T
    line = jnp.concatenate([line[:64], line[64:]], 1)
    line = line * jnp.where((lane_of((ROWS, N)) & 127) == SLABS - TURN, 1.0 / (N * N), 2.0 / (N * N))
    high, low = split(line)
    both = dot(jnp.concatenate([high, low], 0), fwd_high[...])
    values = both[:ROWS] + (both[ROWS:] + dot(high, fwd_low[...]))
    result[...] = values
    leave = pltpu.make_async_copy(result, volume, sem)
    leave.start()

    def channels(step, carry):
        for k in range(8):
            c = step * 8 + k
            piece = features[pl.ds(pl.multiple_of(c * ROWS, ROWS), ROWS), :].astype(F32) * values
            piece = sum(piece[z * YP : (z + 1) * YP] for z in range(ZL))
            partial[pl.ds(pl.multiple_of(c * YP, YP), YP), :] = piece[:, :128] + piece[:, 128:]
        return carry

    lax.fori_loop(0, C // 8, channels, 0)
    total = sum(partial[pl.ds(y, C, stride=YP), :] for y in range(YP))
    total = jnp.concatenate([total, jnp.zeros((128 - C, 128), F32)], 0)
    high, low = split(total)
    rest = (total - high.astype(F32) - low.astype(F32)).astype(BF16)
    ones = jnp.ones((sums.shape[0], 128), BF16)
    nt = ((1,), (1,))
    sums[...] = dot(ones, high, nt) + (dot(ones, low, nt) + dot(ones, rest, nt))
    leave.wait()


def call(body, outs, spaces, scratch=(), cost=(0, 0)):
    whole = {"v": pl.BlockSpec(memory_space=pltpu.VMEM), "s": pl.BlockSpec(memory_space=pltpu.SMEM), "h": pl.BlockSpec(memory_space=pltpu.HBM)}
    ins, goals = spaces.split(">")
    return pl.pallas_call(
        body,
        out_shape=[jax.ShapeDtypeStruct(shape, kind) for shape, kind in outs],
        in_specs=[whole[space] for space in ins],
        out_specs=[whole[space] for space in goals],
        scratch_shapes=list(scratch),
        compiler_params=pltpu.CompilerParams(vmem_limit_bytes=VMEM_LIMIT),
        cost_estimate=pl.CostEstimate(flops=cost[0], bytes_accessed=cost[1], transcendentals=0),
    )


def turned_order(size, first):
    return [(first + n) % size for n in range(size)]


def far_first(names, sizes, first):
    dims = [sizes[name] for name in names]
    spots = np.stack(np.unravel_index(np.arange(math.prod(dims)), dims), 1)
    apart = np.abs(spots - spots[first])
    apart = np.minimum(apart, np.array(dims) - apart).sum(1)
    apart[first] = sum(dims)
    return [int(n) for n in np.argsort(-apart, kind="stable")]


def exchange(array, names, order):
    return lax.all_to_all(array, names, 0, 0, axis_index_groups=[order], tiled=True)


def hbm(array):
    return pltpu.with_memory_space_constraint(array, pltpu.HBM)


def on_device(sizes, features, target, out_weight, rotation, blocks, wedge):
    slab = tuple(name for name, _ in PARTS["slab"])
    features = features.reshape(C * ROWS, N)
    target = target.reshape(ROWS, N)
    fwd_high, fwd_low, along_high, along_low = [hbm(jnp.asarray(table)) for table in tables()]
    lines, features, fwd_high, fwd_low = call(
        forward_x,
        [((128, 128), F32), ((C * ROWS, N), BF16), (fwd_high.shape, BF16), (fwd_low.shape, BF16)],
        "hhhhh>vvvv",
        [pltpu.SMEM((C,), F32), pltpu.VMEM((ROWS, N), BF16), pltpu.SemaphoreType.DMA((4 + CHUNKS,))],
        (200_000_000, 3_000_000),
    )(hbm(out_weight), hbm(target), hbm(features), fwd_high, fwd_low)
    rotation, lines = lax.optimization_barrier((rotation, lines))
    factors, along_high, along_low = call(
        prepare,
        [((N, 128), F32), (along_high.shape, BF16), (along_low.shape, BF16)],
        "shhhh>vvv",
        [pltpu.SMEM((2, NB), jnp.int32), pltpu.VMEM((N, N), jnp.int32), pltpu.SemaphoreType.DMA((4,))],
        (200_000_000, 3_000_000),
    )(rotation, hbm(blocks.T), hbm(wedge), along_high, along_low)
    lines = exchange(lines.reshape(SLABS, 4, 128), slab, turned_order(SLABS, TURN)).reshape(128, 128)
    (back,) = call(filter_z, [((128, 128), F32)], "vvvv>v", (), (200_000_000, 2_000_000))(
        lines, factors, along_high, along_low
    )
    back = exchange(back.reshape(SLABS, 4, 128), slab, turned_order(SLABS, TURN)).reshape(128, 128)
    far = math.prod(sizes[name] for name in FAR)
    near = math.prod(sizes[name] for name in NEAR)
    volume, sums = call(
        inverse_x,
        [((ROWS, N), F32), ((far, 128), F32)],
        "vvvv>hv",
        [pltpu.VMEM((ROWS, N), F32), pltpu.VMEM((C * YP, 128), F32), pltpu.SemaphoreType.DMA],
        (200_000_000, 3_000_000),
    )(back, features, fwd_high, fwd_low)
    sums = exchange(sums.reshape(far, 1, 128), FAR, far_first(FAR, sizes, FIRST_FAR % far))
    sums = jnp.sum(sums, 0, keepdims=True)
    sums = jnp.broadcast_to(sums, (near, 1, 128))
    sums = exchange(sums, NEAR, far_first(NEAR, sizes, FIRST_NEAR % near))
    w_grad = jnp.sum(sums, (0, 1))[:C] * (1.0 / (math.prod(sizes.values()) * ROWS * N))
    return volume.reshape(1, ZL, YP, N), w_grad


def solution(mesh):
    parts = PARTS["dp"] + PARTS["slab"]
    sizes = dict(parts)
    dp = tuple(name for name, _ in PARTS["dp"])
    slab = tuple(name for name, _ in PARTS["slab"])
    fine = Mesh(mesh.devices.reshape([size for _, size in parts]), tuple(sizes))
    in_specs = (P(dp, None, slab, None, None), P(dp, slab, None, None), P(), P(dp), P(), P())
    out_specs = (P(dp, slab, None, None), P())
    return jax.shard_map(
        functools.partial(on_device, sizes), mesh=fine, in_specs=in_specs, out_specs=out_specs, check_vma=False
    )
```

```python
import functools
import math

import jax
import jax.numpy as jnp
import numpy as np
from jax import lax
from jax.experimental import pallas as pl
from jax.experimental.pallas import tpu as pltpu
from jax.sharding import Mesh
from jax.sharding import PartitionSpec as P

N = 256
C = 64
BLK = 64
NB = 8
SLABS = 32
ZL = 8
YP = 8
ROWS = ZL * YP
CHUNKS = 8
PARTS = {"dp": (("y", 4), ("xh", 2), ("core", 2)), "slab": (("z", 16), ("xl", 2))}
NEAR = ("y", "xh", "xl")
FAR = ("core", "z")
TURN = SLABS // 2 + 1
FIRST_FAR = 24
FIRST_NEAR = 11

F32, BF16 = jnp.float32, jnp.bfloat16
VMEM_LIMIT = 16 * 1024 * 1024


def halves(table):
    high = table.astype(np.float32).astype(BF16)
    low = (table - high.astype(np.float64)).astype(np.float32).astype(BF16)
    return high, low


def tables():
    step = 2.0 * math.pi / N
    space = np.arange(N)
    quad, slab = np.meshgrid(np.arange(4), np.arange(SLABS), indexing="ij")
    freq = (4 * ((slab + TURN) % SLABS) + quad).reshape(-1)
    phase = (freq[:, None] * space[None, :]) % N * step
    real, imag = np.cos(phase), -np.sin(phase)
    imag[freq == 0] = np.cos(math.pi * space)
    zp, m, i = np.meshgrid(np.arange(2), np.arange(4), np.arange(SLABS), indexing="ij")
    depth = (8 * ((i + TURN) % SLABS) + 2 * m + zp).reshape(-1)
    phase = (depth[:, None] * depth[None, :]) % N * step
    along = np.concatenate([np.cos(phase), np.sin(phase)], 0)
    return halves(np.concatenate([real, imag], 0)) + halves(along)


def split(values):
    high = values.astype(BF16)
    return high, (values - high.astype(F32)).astype(BF16)


def dot(left, right, dims=((1,), (0,))):
    return lax.dot_general(left, right, (dims, ((), ())), preferred_element_type=F32)


def lane_of(shape):
    return lax.broadcasted_iota(jnp.int32, shape, 1)


def regroup(pieces, to):
    group = (lane_of(pieces[0].shape) >> 4) & 3
    result = None
    for source in range(4):
        moved = pieces[source] if source == to else pltpu.roll(pieces[source], (16 * (source - to)) % 128, 1)
        result = moved if result is None else jnp.where(group == source, moved, result)
    return result


def slab_index():
    return lax.axis_index(tuple(name for name, _ in PARTS["slab"])).astype(jnp.int32)


def filter_weights(turn, place, blocks, wedge, out):
    kz = lax.broadcasted_iota(jnp.int32, (8, N), 0)
    kx = lane_of((8, N)) >> 6
    listed = jnp.zeros((8, N), jnp.bool_)
    for n in range(NB):
        listed = listed | ((kz == blocks[0, n]) & (kx == blocks[1, n]))
    listed = listed.astype(F32)
    mask = jnp.concatenate(
        [wedge[a * BLK : (a + 1) * BLK, :].astype(F32) * listed[a : a + 1, :] for a in range(N // BLK)], 0
    ).astype(BF16)
    lane = lane_of((N, 128))
    row = lax.broadcasted_iota(jnp.int32, (N, 128), 0)
    quad = (lane >> 4) & 3
    freq = 4 * place + quad
    freq = jnp.where((freq == 0) & (lane >= 64), N // 2, freq)
    plus = (row == freq).astype(F32).astype(BF16)
    minus = (row == ((N - freq) & (N - 1))).astype(F32).astype(BF16)
    picks = jnp.concatenate([plus, minus], 1)
    odd = (turn & 1) == 1
    plain = dot(mask, picks)
    other = dot(mask, picks, ((0,), (0,)))
    direct = jnp.where(odd, other[:, 128:], plain[:, :128])
    mirror = jnp.where(odd, other[:, :128], plain[:, 128:]).astype(BF16)
    r = lax.broadcasted_iota(jnp.int32, (N, N), 0)
    p = (8 * ((r & 31) + TURN) + 2 * ((r >> 5) & 3) + (r >> 7)) & (N - 1)
    k = lane_of((N, N))
    keep = (k == p).astype(F32).astype(BF16)
    flip = (((p + k) & (N - 1)) == 0).astype(F32).astype(BF16)
    out[...] = dot(keep, direct.astype(BF16)) + dot(flip, mirror)


def prepare(turn, blocks_hbm, wedge_hbm, high_hbm, low_hbm, factors, high, low, blocks, wedge, sems):
    pairs = [(blocks_hbm, blocks), (wedge_hbm, wedge), (high_hbm, high), (low_hbm, low)]
    copies = [pltpu.make_async_copy(source, goal, sems.at[n]) for n, (source, goal) in enumerate(pairs)]
    for copy in copies:
        copy.start()
    for copy in copies[:2]:
        copy.wait()
    filter_weights(turn[0], slab_index(), blocks, wedge, factors)
    for copy in copies[2:]:
        copy.wait()


def forward_x(weight_hbm, target_hbm, features_hbm, high_hbm, low_hbm, lines, features, fwd_high, fwd_low, weight, target, sems):
    part = C * ROWS // CHUNKS
    pairs = [(weight_hbm, weight), (target_hbm, target)]
    for k in range(CHUNKS):
        rows = pl.ds(k * part, part)
        pairs.append((features_hbm.at[rows], features.at[rows]))
    pairs += [(high_hbm, fwd_high), (low_hbm, fwd_low)]
    copies = [pltpu.make_async_copy(source, goal, sems.at[n]) for n, (source, goal) in enumerate(pairs)]
    for copy in copies:
        copy.start()
    for copy in copies[:2]:
        copy.wait()
    total = -target[...].astype(F32)
    for k in range(CHUNKS):
        copies[2 + k].wait()
        for c in range(k * C // CHUNKS, (k + 1) * C // CHUNKS):
            total = total + weight[c] * features[c * ROWS : (c + 1) * ROWS, :].astype(F32)
    high, low = split(total)
    nt = ((1,), (1,))
    for copy in copies[2 + CHUNKS :]:
        copy.wait()
    both = dot(fwd_high[...], jnp.concatenate([high, low], 0), nt)
    line = dot(fwd_low[...], jnp.concatenate([high, high], 0), nt) + (both + pltpu.roll(both, 64, 1))
    line = jnp.where(lane_of((128, 128)) < 64, line[:128], line[128:])
    pieces = [line[q * SLABS : (q + 1) * SLABS] for q in range(4)]
    for m in range(4):
        lines[pl.ds(m, SLABS, stride=4), :] = regroup(pieces, m)


def three(left_high, left_low, right):
    high, low = split(right)
    both = dot(left_high, jnp.concatenate([high, low], 1))
    return dot(left_low, high) + (both[:, :128] + both[:, 128:])


def filter_z(lines, factors, along_high, along_low, back):
    even = jnp.concatenate([lines[pl.ds(m, SLABS, stride=4), :] for m in range(4)], 0)
    data = jnp.concatenate([even, pltpu.roll(even, 120, 1)], 0)
    freq = three(along_high[...], along_low[...], data)
    cosine, sine = freq[:N], freq[N:]
    lane = lane_of((N, 128))
    sign = jnp.where(lane < 64, 1.0, -1.0)
    sign = jnp.where((slab_index() == 0) & (((lane >> 4) & 3) == 0), 0.0, sign)
    scale = factors[...]
    kept_cosine = scale * (cosine + sign * pltpu.roll(sine, 64, 1))
    kept_sine = scale * (sine - sign * pltpu.roll(cosine, 64, 1))
    depth = three(along_high[:N, :], along_low[:N, :], kept_cosine) + three(along_high[N:, :], along_low[N:, :], kept_sine)
    lane = lane_of((SLABS, 128))
    for m in range(4):
        first = depth[m * SLABS : (m + 1) * SLABS]
        second = depth[128 + m * SLABS : 128 + (m + 1) * SLABS]
        back[pl.ds(m, SLABS, stride=4), :] = jnp.where((lane & 8) == 0, first, pltpu.roll(second, 8, 1))


def inverse_x(lines, features, fwd_high, fwd_low, volume, sums, result, partial, sem):
    blocks = [lines[pl.ds(m, SLABS, stride=4), :] for m in range(4)]
    line = jnp.concatenate([regroup(blocks, q) for q in range(4)], 0).T
    line = jnp.concatenate([line[:64], line[64:]], 1)
    line = line * jnp.where((lane_of((ROWS, N)) & 127) == SLABS - TURN, 1.0 / (N * N), 2.0 / (N * N))
    high, low = split(line)
    both = dot(jnp.concatenate([high, low], 0), fwd_high[...])
    values = both[:ROWS] + (both[ROWS:] + dot(high, fwd_low[...]))
    result[...] = values
    leave = pltpu.make_async_copy(result, volume, sem)
    leave.start()

    def channels(step, carry):
        for k in range(8):
            c = step * 8 + k
            piece = features[pl.ds(pl.multiple_of(c * ROWS, ROWS), ROWS), :].astype(F32) * values
            piece = sum(piece[z * YP : (z + 1) * YP] for z in range(ZL))
            partial[pl.ds(pl.multiple_of(c * YP, YP), YP), :] = piece[:, :128] + piece[:, 128:]
        return carry

    lax.fori_loop(0, C // 8, channels, 0)
    total = sum(partial[pl.ds(y, C, stride=YP), :] for y in range(YP))
    total = jnp.concatenate([total, jnp.zeros((128 - C, 128), F32)], 0)
    high, low = split(total)
    rest = (total - high.astype(F32) - low.astype(F32)).astype(BF16)
    ones = jnp.ones((sums.shape[0], 128), BF16)
    nt = ((1,), (1,))
    sums[...] = dot(ones, high, nt) + (dot(ones, low, nt) + dot(ones, rest, nt))
    leave.wait()


def call(body, outs, spaces, scratch=(), cost=(0, 0)):
    whole = {"v": pl.BlockSpec(memory_space=pltpu.VMEM), "s": pl.BlockSpec(memory_space=pltpu.SMEM), "h": pl.BlockSpec(memory_space=pltpu.HBM)}
    ins, goals = spaces.split(">")
    return pl.pallas_call(
        body,
        out_shape=[jax.ShapeDtypeStruct(shape, kind) for shape, kind in outs],
        in_specs=[whole[space] for space in ins],
        out_specs=[whole[space] for space in goals],
        scratch_shapes=list(scratch),
        compiler_params=pltpu.CompilerParams(vmem_limit_bytes=VMEM_LIMIT),
        cost_estimate=pl.CostEstimate(flops=cost[0], bytes_accessed=cost[1], transcendentals=0),
    )


def turned_order(size, first):
    return [(first + n) % size for n in range(size)]


def far_first(names, sizes, first):
    dims = [sizes[name] for name in names]
    spots = np.stack(np.unravel_index(np.arange(math.prod(dims)), dims), 1)
    apart = np.abs(spots - spots[first])
    apart = np.minimum(apart, np.array(dims) - apart).sum(1)
    apart[first] = sum(dims)
    return [int(n) for n in np.argsort(-apart, kind="stable")]


def exchange(array, names, order):
    return lax.all_to_all(array, names, 0, 0, axis_index_groups=[order], tiled=True)


def hbm(array):
    return pltpu.with_memory_space_constraint(array, pltpu.HBM)


def on_device(sizes, features, target, out_weight, rotation, blocks, wedge):
    slab = tuple(name for name, _ in PARTS["slab"])
    features = features.reshape(C * ROWS, N)
    target = target.reshape(ROWS, N)
    fwd_high, fwd_low, along_high, along_low = [hbm(jnp.asarray(table)) for table in tables()]
    lines, features, fwd_high, fwd_low = call(
        forward_x,
        [((128, 128), F32), ((C * ROWS, N), BF16), (fwd_high.shape, BF16), (fwd_low.shape, BF16)],
        "hhhhh>vvvv",
        [pltpu.SMEM((C,), F32), pltpu.VMEM((ROWS, N), BF16), pltpu.SemaphoreType.DMA((4 + CHUNKS,))],
        (200_000_000, 3_000_000),
    )(hbm(out_weight), hbm(target), hbm(features), fwd_high, fwd_low)
    rotation, lines = lax.optimization_barrier((rotation, lines))
    factors, along_high, along_low = call(
        prepare,
        [((N, 128), F32), (along_high.shape, BF16), (along_low.shape, BF16)],
        "shhhh>vvv",
        [pltpu.SMEM((2, NB), jnp.int32), pltpu.VMEM((N, N), jnp.int32), pltpu.SemaphoreType.DMA((4,))],
        (200_000_000, 3_000_000),
    )(rotation, hbm(blocks.T), hbm(wedge), along_high, along_low)
    lines = exchange(lines.reshape(SLABS, 4, 128), slab, turned_order(SLABS, TURN)).reshape(128, 128)
    (back,) = call(filter_z, [((128, 128), F32)], "vvvv>v", (), (200_000_000, 2_000_000))(
        lines, factors, along_high, along_low
    )
    back = exchange(back.reshape(SLABS, 4, 128), slab, turned_order(SLABS, TURN)).reshape(128, 128)
    far = math.prod(sizes[name] for name in FAR)
    near = math.prod(sizes[name] for name in NEAR)
    volume, sums = call(
        inverse_x,
        [((ROWS, N), F32), ((far, 128), F32)],
        "vvvv>hv",
        [pltpu.VMEM((ROWS, N), F32), pltpu.VMEM((C * YP, 128), F32), pltpu.SemaphoreType.DMA],
        (200_000_000, 3_000_000),
    )(back, features, fwd_high, fwd_low)
    sums = exchange(sums.reshape(far, 1, 128), FAR, far_first(FAR, sizes, FIRST_FAR % far))
    sums = jnp.sum(sums, 0, keepdims=True)
    sums = jnp.broadcast_to(sums, (near, 1, 128))
    sums = exchange(sums, NEAR, far_first(NEAR, sizes, FIRST_NEAR % near))
    w_grad = jnp.sum(sums, (0, 1))[:C] * (1.0 / (math.prod(sizes.values()) * ROWS * N))
    return volume.reshape(1, ZL, YP, N), w_grad


def solution(mesh):
    parts = PARTS["dp"] + PARTS["slab"]
    sizes = dict(parts)
    dp = tuple(name for name, _ in PARTS["dp"])
    slab = tuple(name for name, _ in PARTS["slab"])
    fine = Mesh(mesh.devices.reshape([size for _, size in parts]), tuple(sizes))
    in_specs = (P(dp, None, slab, None, None), P(dp, slab, None, None), P(), P(dp), P(), P())
    out_specs = (P(dp, slab, None, None), P())
    return jax.shard_map(
        functools.partial(on_device, sizes), mesh=fine, in_specs=in_specs, out_specs=out_specs, check_vma=False
    )
```
